32 devices in a mesh: grp: 4 (over y, x), ctx: 8 (over z, core).
Axes of the slice: x: 2, y: 2, z: 4, core: 2. Of those that a mesh axis runs over, the one named last changes fastest.
Arguments:
- tokens: bfloat16 [4096, 2048], P(('grp', 'ctx')), may hold values from -3 to 3
- queries: bfloat16 [4096, 4096], P(('grp', 'ctx')), may hold values from -6 to 6
- keys_values: bfloat16 [4, 2048, 1024], P('grp', 'ctx'), may hold values from -600 to 600
- out_weight: bfloat16 [4096, 2048], P('grp'), may hold values from -1 to 1
- moe_gain: float32 [2048], replicated, may hold values from 0.1 to 1.9
- expert_ids: int32 [4096, 8], P(('grp', 'ctx')), may hold values from 0 to 127, all different within a row; in each aligned block of 128 rows (0 to 127, 128 to 255, ...) at most 12 rows name the same one
- gates: float32 [4096, 8], P(('grp', 'ctx')), may hold values from 0.05 to 0.3
- w_gate_experts: bfloat16 [128, 2048, 768], P(('grp', 'ctx')), may hold values from -0.125 to 0.125
- w_up_experts: bfloat16 [128, 2048, 768], P(('grp', 'ctx')), may hold values from -0.125 to 0.125
- w_down_experts: bfloat16 [128, 768, 2048], P(('grp', 'ctx')), may hold values from -0.21875 to 0.21875
Outputs:
- layer_out: bfloat16 [4096, 2048], P(('grp', 'ctx'))
The draws below stay inside these ranges and needn't reach their ends.
Inputs may be any that keep to these rules, and one draw needn't show every extreme that they name: `expert_ids`: each row names 8 different experts; among the 128 rows of one device no expert is named more than 12 times, a bound that some block reaches.
All inputs are finite; a program needn't handle non-finite values.
Results may differ from the reference program's by a relative error of at most 0.015.
Values may be sent and summed in bfloat16 or wider, within the bound.
No kernel may reach another device: no remote copies, remote signals or barrier semaphores. Data moves between devices by JAX's collectives and lax.ppermute only.
A program may use at most 128 MiB of HBM per device.

```python
import math
import jax
import jax.numpy as jnp
import numpy as np
from jax import lax

D = 2048
H = 32
KV_HEADS = 4
HEAD_DIM = 128
FF = 768
EXPERTS = 128
TOPK = 8
TOK_DEV = 128
CAP = 12
KEYS = 2048
SEQS = 4
TOKENS = 4096


def draw_keys_values(key, part):
    width = KV_HEADS * HEAD_DIM
    first_key = jax.random.fold_in(jax.random.fold_in(key, 17), 0)
    drawn = jnp.clip(jax.random.normal(first_key, (SEQS, KEYS, 2 * width), jnp.float32), -5.0, 5.0)
    return drawn.astype(jnp.bfloat16)


def block_scale(own_key, dims, cuts, smallest, high):
    level, own = 1.0, jax.random.fold_in(own_key, 6)
    for dim, blocks in cuts:
        steps = jnp.exp(jax.random.uniform(jax.random.fold_in(own, dim), (blocks,), jnp.float32, smallest / len(cuts), high / len(cuts)))
        level = level * jnp.repeat(steps, dims[dim] // blocks).reshape([-1 if axis == dim else 1 for axis in range(len(dims))])
    return level


def routed_block(own_key, own, number, rows, amount, top, reach, skew):
    order = jax.random.permutation(own_key, amount)
    crowded, common = shares(amount, rows * top, reach, skew, True), shares(amount, rows * top, reach, skew, False)
    places = jnp.arange(amount)

    def named(lengths, rotation):
        used = int((lengths > 0).sum())
        fixed = max(1, used // 4)
        moved = fixed + (places - fixed + rotation * (used - fixed)) % max(1, amount - fixed)
        return jnp.zeros((amount,), jnp.int32).at[order[jnp.where(places < fixed, places, moved)]].set(jnp.asarray(lengths, jnp.int32))

    lengths = jnp.where(number % 4 == 0, named(crowded, number // 4), named(common, number - number // 4 - 1))
    mixed = jax.random.permutation(jax.random.fold_in(own, 3), amount)
    donor, receiver = mixed[0:amount // 2 * 2:2], mixed[1:amount // 2 * 2:2]
    margin = jnp.minimum(lengths[donor] - 1, reach - lengths[receiver]) // 2
    margin = jnp.where((donor == order[0]) | (receiver == order[0]) | (lengths[receiver] == 0), 0, jnp.maximum(margin, 0))
    moved = jax.random.randint(jax.random.fold_in(own, 4), (amount // 2,), 0, 1 << 20) % (margin + 1)
    lengths = lengths.at[donor].add(-moved).at[receiver].add(moved)
    labels = jnp.searchsorted(jnp.cumsum(lengths), jnp.arange(rows * top), side="right").astype(jnp.int32)
    table = labels.reshape(top, rows).T
    table = table[jax.random.permutation(jax.random.fold_in(own, 1), rows)]
    rotation = jax.random.randint(jax.random.fold_in(own, 2), (rows, 1), 0, top)
    return jnp.take_along_axis(table, (jnp.arange(top)[None, :] + rotation) % top, axis=1)


def shares(count, total, most, slope, full):
    weights = [(1 << 20) // math.isqrt(standing ** slope) + 1 for standing in range(1, count + 1)]
    largest = most if full else min(most, max(-(-total // count), total * weights[0] // sum(weights)))
    least = 1 if total - largest >= count - 1 else 0
    counts, spare = [largest] + [least] * (count - 1), total - largest - least * (count - 1)
    while spare > 0:
        candidates = [i for i in range(1, count) if counts[i] < largest] or [i for i in range(1, count) if counts[i] < most]
        mass, remaining = sum([weights[i] for i in candidates]), spare
        for i in candidates:
            more = min(most - counts[i], max(1, remaining * weights[i] // mass), spare)
            counts[i] = counts[i] + more
            spare = spare - more
    return np.array(counts)


def gaussian(stream_key, dims, deviation, most, pieces=(), held_as=jnp.bfloat16):
    gain = block_scale(stream_key, dims, pieces, -0.22, 0.18) if pieces else 1.0
    entries = jax.random.normal(stream_key, dims, jnp.float32) * deviation * gain
    return jnp.minimum(jnp.maximum(entries, -most), most).astype(held_as)


def setup_inputs(seed: int = 0) -> dict:
    key_of = jax.random.split(jax.random.key(seed), 11)
    tokens = gaussian(key_of[0], (TOKENS, D), 0.5, 3.0, ((0, 32),))
    queries = gaussian(key_of[1], (TOKENS, H * HEAD_DIM), 1.0, 6.0, ((0, 32),))
    keys_values = draw_keys_values(jax.random.fold_in(key_of[10], 71), 0)
    out_weight = gaussian(key_of[3], (H * HEAD_DIM, D), (H * HEAD_DIM // 128) ** -0.5, 1.0, ((0, 4),))
    moe_gain = jnp.clip(1.0 + 0.18 * jax.random.normal(key_of[4], (D,), jnp.float32), 0.1, 1.9)
    expert_ids_keys = jax.random.split(jax.random.fold_in(key_of[5], 1), TOKENS // TOK_DEV)
    expert_ids_turns = jax.random.permutation(jax.random.fold_in(key_of[5], 3), TOKENS // TOK_DEV)
    expert_ids = jax.vmap(lambda own, number: routed_block(jax.random.fold_in(key_of[5], 2), own, number, TOK_DEV, EXPERTS, TOPK, CAP, 2))(expert_ids_keys, expert_ids_turns).reshape((TOKENS, TOPK))
    gates = jnp.clip(0.05 + 0.25 * jax.random.uniform(key_of[6], (TOKENS, TOPK), jnp.float32) ** block_scale(key_of[6], (TOKENS, TOPK), ((0, 32),), -0.2, 0.2), 0.05, 0.3)
    w_gate_experts = gaussian(key_of[7], (EXPERTS, D, FF), D ** -0.5, 0.125, ((0, 32),))
    w_up_experts = gaussian(key_of[8], (EXPERTS, D, FF), D ** -0.5, 0.125, ((0, 32),))
    w_down_experts = gaussian(key_of[9], (EXPERTS, FF, D), FF ** -0.5, 0.21875, ((0, 32),))
    return dict(tokens=tokens, queries=queries, keys_values=keys_values, out_weight=out_weight, moe_gain=moe_gain, expert_ids=expert_ids, gates=gates, w_gate_experts=w_gate_experts, w_up_experts=w_up_experts, w_down_experts=w_down_experts)


masked_score = -1e+30

def sequence_attention(query_seq, kv_seq):
    new_count = query_seq.shape[0]
    key_count = kv_seq.shape[0]
    width = KV_HEADS * HEAD_DIM
    group_heads = H // KV_HEADS
    scaling = 1.0 / math.sqrt(HEAD_DIM)
    query_position = key_count - new_count + jnp.arange(new_count, dtype=jnp.int32)
    key_position = jnp.arange(key_count, dtype=jnp.int32)
    allowed = jnp.tile(key_position[None, :] <= query_position[:, None], (group_heads, 1))
    key_heads = kv_seq[:, :width].reshape(key_count, KV_HEADS, HEAD_DIM).transpose(1, 0, 2)
    value_heads = kv_seq[:, width:].reshape(key_count, KV_HEADS, HEAD_DIM).transpose(1, 0, 2)
    query_heads = query_seq.reshape(new_count, KV_HEADS, group_heads, HEAD_DIM).transpose(1, 2, 0, 3).reshape(KV_HEADS, group_heads * new_count, HEAD_DIM)

    def one_head(inputs):
        query_rows, key_rows, value_rows = inputs
        scores = jnp.dot(query_rows, key_rows.T, preferred_element_type=jnp.float32) * scaling
        scores = jnp.where(allowed, scores, masked_score)
        top_score = lax.optimization_barrier(jnp.max(scores, axis=1, keepdims=True))
        weights = jnp.where(allowed, jnp.exp(scores - top_score), 0.0).astype(jnp.bfloat16)
        total = lax.optimization_barrier(jnp.sum(weights.astype(jnp.float32), axis=1, keepdims=True))
        return jnp.dot(weights, value_rows, preferred_element_type=jnp.float32) / total
    outputs = lax.map(one_head, (query_heads, key_heads, value_heads))
    return outputs.reshape(KV_HEADS, group_heads, new_count, HEAD_DIM).transpose(2, 0, 1, 3).reshape(new_count, H * HEAD_DIM).astype(jnp.bfloat16)

def run_sequence(inputs):
    return sequence_attention(inputs[0], inputs[1])

def reference(tokens, queries, keys_values, out_weight, moe_gain, expert_ids, gates, w_gate_experts, w_up_experts, w_down_experts):
    query_seqs = queries.reshape(SEQS, TOKENS // SEQS, H * HEAD_DIM)
    attended = lax.map(run_sequence, (query_seqs, keys_values)).reshape(TOKENS, H * HEAD_DIM)
    projected = jnp.dot(attended, out_weight, preferred_element_type=jnp.float32)
    residual = (tokens.astype(jnp.float32) + projected).astype(jnp.bfloat16)
    wide = residual.astype(jnp.float32)
    normed = (wide * lax.rsqrt(lax.optimization_barrier(jnp.mean(wide * wide, axis=1, keepdims=True)) + 1e-06) * moe_gain).astype(jnp.bfloat16)
    block_count = TOKENS // TOK_DEV
    assigned = expert_ids.reshape(block_count, TOK_DEV * TOPK)
    one_hot = (assigned[:, :, None] == jnp.arange(EXPERTS, dtype=jnp.int32)[None, None, :]).astype(jnp.int32)
    earlier = jnp.cumsum(one_hot, axis=1) - one_hot
    slot_index = lax.optimization_barrier(jnp.sum(earlier * one_hot, axis=2))
    block_index = jnp.arange(block_count, dtype=jnp.int32)[:, None]
    position = (assigned * (block_count * CAP) + block_index * CAP + slot_index).reshape(-1).astype(jnp.int32)
    token_index = jnp.arange(TOKENS * TOPK, dtype=jnp.int32) // TOPK
    table = jnp.full((EXPERTS * block_count * CAP,), TOKENS, jnp.int32).at[position].set(token_index).reshape(EXPERTS, block_count * CAP)

    def run_expert(inputs):
        table_row, gate_matrix, up_matrix, down_matrix = inputs
        present = table_row < TOKENS
        gathered = jnp.where(present[:, None], normed[jnp.minimum(table_row, TOKENS - 1)], 0.0).astype(jnp.bfloat16)
        gate_part = jnp.dot(gathered, gate_matrix, preferred_element_type=jnp.float32)
        up_part = jnp.dot(gathered, up_matrix, preferred_element_type=jnp.float32)
        hidden = (jax.nn.silu(gate_part) * up_part).astype(jnp.bfloat16)
        return jnp.dot(hidden, down_matrix, preferred_element_type=jnp.float32).astype(jnp.bfloat16)
    expert_outputs = lax.map(run_expert, (table, w_gate_experts, w_up_experts, w_down_experts))
    picked = expert_outputs.reshape(EXPERTS * block_count * CAP, D)[position].reshape(TOKENS, TOPK, D)
    combined = lax.optimization_barrier(jnp.sum(picked.astype(jnp.float32) * gates[:, :, None], axis=1))
    return (residual.astype(jnp.float32) + combined).astype(jnp.bfloat16)
```

```python
import functools
import math

import jax
import jax.numpy as jnp
from jax import lax
from jax.experimental import pallas as pl
from jax.experimental.pallas import tpu as pltpu
from jax.sharding import PartitionSpec as P

H = 32
KV_HEADS = 4
HEAD_DIM = 128
EXPERTS = 128
TOPK = 8
CAP = 12

CHUNKS = 2
VMEM_LIMIT = 56 * 1024 * 1024


def attention_kernel(base_ref, q_ref, k_ref, v_ref, o_ref, *, heads, stack, old):
    rows = q_ref.shape[0]
    keys = k_ref.shape[0]
    factor = math.log2(math.e) / math.sqrt(HEAD_DIM)
    key = k_ref[...]
    value = jnp.concatenate([v_ref[...], jnp.ones_like(v_ref)], axis=1)
    late = (stack * rows, keys - old)
    row = lax.broadcasted_iota(jnp.int32, late, 0) % rows
    allowed = lax.broadcasted_iota(jnp.int32, late, 1) + old <= row + base_ref[0]
    for first in range(0, heads, stack):
        query = jnp.concatenate(
            [q_ref[:, h * HEAD_DIM : (h + 1) * HEAD_DIM] for h in range(first, first + stack)],
            axis=0,
        )
        scores = lax.dot_general(
            query, key, (((1,), (1,)), ((), ())), preferred_element_type=jnp.float32
        )
        scores = jnp.concatenate(
            [scores[:, :old], jnp.where(allowed, scores[:, old:], -1e30)], axis=1
        )
        top = jnp.max(scores, axis=1, keepdims=True)
        weights = jnp.exp2((scores - top) * factor).astype(jnp.bfloat16)
        summed = jnp.dot(weights, value, preferred_element_type=jnp.float32)
        out = (summed[:, :HEAD_DIM] / summed[:, HEAD_DIM:]).astype(o_ref.dtype)
        for i in range(stack):
            h = first + i
            o_ref[:, h * HEAD_DIM : (h + 1) * HEAD_DIM] = out[i * rows : (i + 1) * rows]


def attention(queries, keys_values, base, old):
    rows = queries.shape[0]
    keys = keys_values.shape[0]
    heads = H // KV_HEADS
    wide = heads * HEAD_DIM
    return pl.pallas_call(
        functools.partial(attention_kernel, heads=heads, stack=2, old=old),
        grid=(KV_HEADS,),
        in_specs=[
            pl.BlockSpec(memory_space=pltpu.SMEM),
            pl.BlockSpec((rows, wide), lambda j: (0, j)),
            pl.BlockSpec((keys, HEAD_DIM), lambda j: (0, j)),
            pl.BlockSpec((keys, HEAD_DIM), lambda j: (0, KV_HEADS + j)),
        ],
        out_specs=pl.BlockSpec((rows, wide), lambda j: (0, j)),
        out_shape=jax.ShapeDtypeStruct(queries.shape, jnp.bfloat16),
        compiler_params=pltpu.CompilerParams(vmem_limit_bytes=VMEM_LIMIT),
        cost_estimate=pl.CostEstimate(
            flops=4 * rows * H * keys * HEAD_DIM,
            bytes_accessed=2 * keys_values.size + 4 * queries.size,
            transcendentals=rows * H * keys,
        ),
        name="attention",
    )(base, queries, keys_values, keys_values)


def hidden_kernel(*refs, peers, chunks):
    x_refs = refs[: peers * chunks]
    gate_ref, up_ref, h_ref = refs[peers * chunks :]
    gate = up = None
    for c in range(chunks):
        part = jnp.concatenate([x_refs[c * peers + k][0] for k in range(peers)], axis=0)
        width = part.shape[1]
        span = slice(c * width, (c + 1) * width)
        g = jnp.dot(part, gate_ref[0, span, :], preferred_element_type=jnp.float32)
        u = jnp.dot(part, up_ref[0, span, :], preferred_element_type=jnp.float32)
        gate = g if gate is None else gate + g
        up = u if up is None else up + u
    h_ref[0] = (gate / (1.0 + jnp.exp(-gate)) * up).astype(h_ref.dtype)


def expert_hidden(parts, w_gate, w_up):
    chunks, peers = len(parts), len(parts[0])
    local, slots, width = parts[0][0].shape
    depth, inner = w_gate.shape[1:]
    rows = peers * slots
    return pl.pallas_call(
        functools.partial(hidden_kernel, peers=peers, chunks=chunks),
        grid=(local,),
        in_specs=[pl.BlockSpec((1, slots, width), lambda j: (j, 0, 0))] * (peers * chunks)
        + [pl.BlockSpec((1, depth, inner), lambda j: (j, 0, 0))] * 2,
        out_specs=pl.BlockSpec((1, rows, inner), lambda j: (j, 0, 0)),
        out_shape=jax.ShapeDtypeStruct((local, rows, inner), jnp.bfloat16),
        compiler_params=pltpu.CompilerParams(vmem_limit_bytes=VMEM_LIMIT),
        cost_estimate=pl.CostEstimate(
            flops=4 * local * rows * depth * inner,
            bytes_accessed=4 * w_gate.size + 2 * local * rows * (depth + inner),
            transcendentals=local * rows * inner,
        ),
        name="expert_hidden",
    )(*[x for part in parts for x in part], w_gate, w_up)


def down_kernel(h_ref, w_ref, *y_refs):
    slots = y_refs[0].shape[1]
    out = jnp.dot(h_ref[0], w_ref[0], preferred_element_type=jnp.float32).astype(jnp.bfloat16)
    for k, y_ref in enumerate(y_refs):
        y_ref[0] = out[k * slots : (k + 1) * slots]


def expert_down(hidden, w_down, chunk, chunks, peers):
    local, rows, inner = hidden.shape
    width = w_down.shape[2] // chunks
    slots = rows // peers
    return pl.pallas_call(
        down_kernel,
        grid=(local,),
        in_specs=[
            pl.BlockSpec((1, rows, inner), lambda j: (j, 0, 0)),
            pl.BlockSpec((1, inner, width), lambda j: (j, 0, chunk)),
        ],
        out_specs=[pl.BlockSpec((1, slots, width), lambda j: (j, 0, 0))] * peers,
        out_shape=[jax.ShapeDtypeStruct((local, slots, width), jnp.bfloat16)] * peers,
        compiler_params=pltpu.CompilerParams(vmem_limit_bytes=VMEM_LIMIT),
        cost_estimate=pl.CostEstimate(
            flops=2 * local * rows * width * inner,
            bytes_accessed=2 * local * (inner * width + rows * (inner + width)),
            transcendentals=0,
        ),
        name="expert_down",
    )(hidden, w_down)


def swap(value, k, peers):
    if k == 0:
        return value
    return lax.ppermute(value, "grp", [(i, i ^ k) for i in range(peers)])


def per_device(
    tokens,
    queries,
    keys_values,
    out_weight,
    moe_gain,
    expert_ids,
    gates,
    w_gate_experts,
    w_up_experts,
    w_down_experts,
):
    tok_count, width = tokens.shape
    ctx_count = lax.axis_size("ctx")
    peers = lax.axis_size("grp")
    here, me = lax.axis_index("ctx"), lax.axis_index("grp")
    local = w_gate_experts.shape[0]
    slots = ctx_count * CAP
    column = ctx_count * tok_count
    chunk_width = width // CHUNKS

    gathered = lax.all_gather(keys_values[0], "ctx", axis=0, tiled=True)
    old = gathered.shape[0] - column
    base = (old + here * tok_count).astype(jnp.int32).reshape(1)
    attended = attention(queries, gathered, base, old)

    packed = jnp.concatenate([expert_ids.astype(jnp.float32), gates], axis=1)
    packed, _ = lax.optimization_barrier((packed, gathered))
    routes = lax.all_gather(packed, "ctx", axis=0, tiled=True).T
    ids, gate_rows = routes[:TOPK].astype(jnp.int32), routes[TOPK:]
    owner = me ^ jnp.arange(peers, dtype=jnp.int32)
    wanted = (
        ((owner * ctx_count + here) * local)[:, None] + jnp.arange(local, dtype=jnp.int32)[None, :]
    ).reshape(-1)
    same = ids[None, :, :] == wanted[:, None, None]
    named = jnp.any(same, axis=1)
    gate_of = jnp.sum(jnp.where(same, gate_rows[None], 0.0), axis=1)
    earlier = jnp.triu(jnp.ones((tok_count, tok_count), jnp.bfloat16), 1)
    rank = jnp.einsum(
        "ebt,tu->ebu",
        named.reshape(-1, ctx_count, tok_count).astype(jnp.bfloat16),
        earlier,
        preferred_element_type=jnp.float32,
    ).astype(jnp.int32)
    place = rank + (jnp.arange(ctx_count, dtype=jnp.int32) * CAP)[None, :, None]
    place = jnp.where(named, place.reshape(-1, column), -1)
    hit = place[:, None, :] == jnp.arange(slots, dtype=jnp.int32)[None, :, None]
    pick = hit.astype(jnp.bfloat16).reshape(peers, local * slots, column)
    mix = jnp.where(hit, gate_of[:, None, :], 0.0).astype(jnp.bfloat16)
    mix = mix.reshape(peers, local * slots, column)

    head_parts = lax.all_to_all(attended, "grp", split_axis=1, concat_axis=0, tiled=True)
    projected = lax.psum_scatter(
        jnp.dot(head_parts, out_weight, preferred_element_type=jnp.float32).astype(jnp.bfloat16),
        "grp",
        scatter_dimension=0,
        tiled=True,
    ).astype(jnp.float32)
    residual = (tokens.astype(jnp.float32) + projected).astype(jnp.bfloat16)
    wide = residual.astype(jnp.float32)
    normed = (
        wide * lax.rsqrt(jnp.mean(wide * wide, axis=1, keepdims=True) + 1e-06) * moe_gain
    ).astype(jnp.bfloat16)

    parts = []
    for c in range(CHUNKS):
        piece = normed[:, c * chunk_width : (c + 1) * chunk_width]
        block = lax.all_gather(piece, "ctx", axis=0, tiled=True)
        received = []
        for k in reversed(range(peers)):
            rows = jnp.dot(pick[k], block, preferred_element_type=jnp.float32)
            received.append(swap(rows.astype(jnp.bfloat16), k, peers))
        parts.append([r.reshape(local, slots, chunk_width) for r in reversed(received)])
    hidden = expert_hidden(parts, w_gate_experts, w_up_experts)

    outs = []
    for c in range(CHUNKS):
        rows = expert_down(hidden, w_down_experts, c, CHUNKS, peers)
        back = [swap(rows[k], k, peers) for k in reversed(range(peers))][::-1]
        total = sum(
            lax.dot_general(
                mix[k],
                back[k].reshape(local * slots, chunk_width),
                (((0,), (0,)), ((), ())),
                preferred_element_type=jnp.float32,
            )
            for k in range(peers)
        ).astype(jnp.bfloat16)
        mine = lax.psum_scatter(total, "ctx", scatter_dimension=0, tiled=True)
        outs.append(wide[:, c * chunk_width : (c + 1) * chunk_width] + mine.astype(jnp.float32))
    return jnp.concatenate(outs, axis=1).astype(jnp.bfloat16)


def solution(mesh):
    return jax.shard_map(
        per_device,
        mesh=mesh,
        in_specs=(
            P(("grp", "ctx"), None),
            P(("grp", "ctx"), None),
            P("grp", "ctx", None),
            P("grp", None),
            P(),
            P(("grp", "ctx"), None),
            P(("grp", "ctx"), None),
            P(("grp", "ctx"), None, None),
            P(("grp", "ctx"), None, None),
            P(("grp", "ctx"), None, None),
        ),
        out_specs=P(("grp", "ctx"), None),
        check_vma=False,
    )
```

```python
import functools
import math

import jax
import jax.numpy as jnp
from jax import lax
from jax.experimental import pallas as pl
from jax.experimental.pallas import tpu as pltpu
from jax.sharding import PartitionSpec as P

H = 32
KV_HEADS = 4
HEAD_DIM = 128
EXPERTS = 128
TOPK = 8
CAP = 12

CHUNKS = 4
VMEM_LIMIT = 48 * 1024 * 1024
VMEM_MOST = 60 * 1024 * 1024


def call(kernel, deps, operands, in_specs, vmem=VMEM_LIMIT, **kwargs):
    count = len(operands)

    def run(*refs):
        kernel(*refs[:count], *refs[count + len(deps) :])

    in_specs = in_specs + [pl.BlockSpec(memory_space=pl.ANY)] * len(deps)
    params = pltpu.CompilerParams(vmem_limit_bytes=vmem)
    if "grid_spec" in kwargs:
        kwargs["grid_spec"] = kwargs["grid_spec"](in_specs)
        in_specs = None
    else:
        kwargs["in_specs"] = in_specs
    return pl.pallas_call(run, compiler_params=params, **kwargs)(*operands, *deps)


def attention_kernel(where_ref, q_ref, *refs, blocks, stack, old):
    k_refs, v_refs = refs[: blocks + 1], refs[blocks + 1 : 2 * blocks + 2]
    o_ref, key_ref, value_ref = refs[2 * blocks + 2 :]
    rows, wide = q_ref.shape
    half = k_refs[1].shape[0]
    keys = key_ref.shape[0]
    factor = math.log2(math.e) / math.sqrt(HEAD_DIM)
    for b in range(blocks):
        lead = slice(2 * b * half, (2 * b + 1) * half)
        part = slice(b * half, (b + 1) * half)
        key_ref[lead, :] = k_refs[0][part, :]
        value_ref[lead, :HEAD_DIM] = v_refs[0][part, :]
        at = pl.ds(pl.multiple_of((2 * where_ref[3 + b] + 1) * half, half), half)
        key_ref[at, :] = k_refs[1 + b][...]
        value_ref[at, :HEAD_DIM] = v_refs[1 + b][...]
    value_ref[:, HEAD_DIM:] = jnp.ones((keys, HEAD_DIM), value_ref.dtype)
    late = (stack * rows, keys - old)
    row = lax.broadcasted_iota(jnp.int32, late, 0) % rows
    allowed = lax.broadcasted_iota(jnp.int32, late, 1) + old <= row + where_ref[2]
    for first in range(0, wide // HEAD_DIM, stack):
        query = jnp.concatenate(
            [q_ref[:, h * HEAD_DIM : (h + 1) * HEAD_DIM] for h in range(first, first + stack)],
            axis=0,
        )
        scores = lax.dot_general(
            query, key_ref[...], (((1,), (1,)), ((), ())), preferred_element_type=jnp.float32
        )
        scores = jnp.concatenate(
            [scores[:, :old], jnp.where(allowed, scores[:, old:], -1e30)], axis=1
        )
        top = jnp.max(scores, axis=1, keepdims=True)
        weights = jnp.exp2((scores - top) * factor).astype(jnp.bfloat16)
        summed = jnp.dot(weights, value_ref[...], preferred_element_type=jnp.float32)
        out = (summed[:, :HEAD_DIM] / summed[:, HEAD_DIM:]).astype(o_ref.dtype)
        for i in range(stack):
            h = first + i
            o_ref[:, h * HEAD_DIM : (h + 1) * HEAD_DIM] = out[i * rows : (i + 1) * rows]


def attention(queries, kv_lead, kv_blocks, where, old, peers, deps):
    rows = queries.shape[0]
    wide = queries.shape[1] // peers
    blocks = len(kv_blocks)
    half = kv_blocks[0].shape[0]
    keys = 2 * half * blocks

    def column(size, first):
        return pl.BlockSpec((size, HEAD_DIM), lambda i, where: (0, first + where[1]))

    sizes = [half * blocks] + [half] * blocks
    return call(
        functools.partial(attention_kernel, blocks=blocks, stack=2, old=old),
        deps,
        [where, queries] + [kv_lead, *kv_blocks] * 2,
        [pl.BlockSpec((rows, wide), lambda i, where: (0, where[0]))]
        + [column(size, 0) for size in sizes]
        + [column(size, KV_HEADS) for size in sizes],
        grid_spec=lambda in_specs: pltpu.PrefetchScalarGridSpec(
            num_scalar_prefetch=1,
            grid=(1,),
            in_specs=in_specs,
            out_specs=pl.BlockSpec((rows, wide), lambda i, where: (0, 0)),
            scratch_shapes=[
                pltpu.VMEM((keys, HEAD_DIM), jnp.bfloat16),
                pltpu.VMEM((keys, 2 * HEAD_DIM), jnp.bfloat16),
            ],
        ),
        out_shape=jax.ShapeDtypeStruct((rows, wide), jnp.bfloat16),
        cost_estimate=pl.CostEstimate(
            flops=4 * rows * wide * keys,
            bytes_accessed=4 * (keys * HEAD_DIM + rows * wide),
            transcendentals=rows * wide // HEAD_DIM * keys,
        ),
        name="attention",
        vmem=VMEM_MOST,
    )


def pick_kernel(order_ref, pick_ref, *refs, blocks):
    if blocks > 1:
        block_refs, outs, scratch = refs[:blocks], refs[blocks:-1], refs[-1]
        span = block_refs[0].shape[0]
        number = 0
        for ref in block_refs:
            for part in range(ref.shape[0] // span):
                at = pl.ds(pl.multiple_of(order_ref[number] * span, span), span)
                scratch[at, :] = ref[part * span : (part + 1) * span, :]
                number += 1
        block = scratch[...]
    else:
        block, outs = refs[0][...], refs[1:]
    count = outs[0].shape[0]
    for k, out in enumerate(outs):
        out[...] = jnp.dot(
            pick_ref[k * count : (k + 1) * count, :], block, preferred_element_type=jnp.float32
        ).astype(out.dtype)


def pick_rows(order, pick, blocks, peers, chunk=0, chunks=1):
    count, width = pick.shape[0] // peers, blocks[0].shape[1] // chunks

    def whole(shape):
        return pl.BlockSpec(shape, lambda i: (0, 0))

    return call(
        functools.partial(pick_kernel, blocks=len(blocks)),
        [],
        [order, pick, *blocks],
        [pl.BlockSpec(memory_space=pltpu.SMEM), whole(pick.shape)]
        + [pl.BlockSpec((b.shape[0], width), lambda i: (0, chunk)) for b in blocks],
        grid=(1,),
        out_specs=[whole((count, width))] * peers,
        out_shape=[jax.ShapeDtypeStruct((count, width), jnp.bfloat16)] * peers,
        scratch_shapes=[pltpu.VMEM((pick.shape[1], width), jnp.bfloat16)] * (len(blocks) > 1),
        cost_estimate=pl.CostEstimate(
            flops=2 * pick.size * width,
            bytes_accessed=2 * (pick.size + (pick.shape[0] + pick.shape[1]) * width),
            transcendentals=0,
        ),
        name="pick_rows",
    )


def hidden_kernel(*refs, peers, carried, last):
    x_refs, refs = refs[:peers], refs[peers:]
    gate_ref, up_ref, *refs = refs
    part = jnp.concatenate([x[...] for x in x_refs], axis=0)
    gate = jnp.dot(part, gate_ref[0], preferred_element_type=jnp.float32)
    up = jnp.dot(part, up_ref[0], preferred_element_type=jnp.float32)
    if carried:
        gate = gate + refs[0][0]
        up = up + refs[1][0]
        refs = refs[2:]
    if last:
        refs[0][0] = (gate / (1.0 + jnp.exp(-gate)) * up).astype(refs[0].dtype)
    else:
        refs[0][0] = gate
        refs[1][0] = up


def expert_hidden(part, first, w_gate, w_up, carry, last, deps=()):
    peers = len(part)
    width = part[0].shape[1]
    local, _, inner = w_gate.shape
    slots = part[0].shape[0] // local
    rows = peers * slots
    assert first % width == 0
    weight_spec = pl.BlockSpec((1, width, inner), lambda j: (j, first // width, 0))
    sum_spec = pl.BlockSpec((1, rows, inner), lambda j: (j, 0, 0))
    total = jax.ShapeDtypeStruct((local, rows, inner), jnp.float32)
    return call(
        functools.partial(hidden_kernel, peers=peers, carried=carry is not None, last=last),
        deps,
        [*part, w_gate, w_up, *(carry or ())],
        [pl.BlockSpec((slots, width), lambda j: (j, 0))] * peers
        + [weight_spec] * 2
        + ([] if carry is None else [sum_spec] * 2),
        grid=(local,),
        out_specs=sum_spec if last else [sum_spec] * 2,
        out_shape=jax.ShapeDtypeStruct(total.shape, jnp.bfloat16) if last else [total] * 2,
        cost_estimate=pl.CostEstimate(
            flops=4 * local * rows * width * inner,
            bytes_accessed=4 * local * width * inner + 10 * local * rows * inner,
            transcendentals=local * rows * inner,
        ),
        name="expert_hidden",
    )


def down_kernel(h_ref, w_ref, *y_refs):
    slots = y_refs[0].shape[0]
    out = jnp.dot(h_ref[0], w_ref[0], preferred_element_type=jnp.float32).astype(jnp.bfloat16)
    for k, y_ref in enumerate(y_refs):
        y_ref[...] = out[k * slots : (k + 1) * slots]


def expert_down(hidden, w_down, chunk, chunks, peers):
    local, rows, inner = hidden.shape
    width = w_down.shape[2] // chunks
    slots = rows // peers
    return pl.pallas_call(
        down_kernel,
        grid=(local,),
        in_specs=[
            pl.BlockSpec((1, rows, inner), lambda j: (j, 0, 0)),
            pl.BlockSpec((1, inner, width), lambda j: (j, 0, chunk)),
        ],
        out_specs=[pl.BlockSpec((slots, width), lambda j: (j, 0))] * peers,
        out_shape=[jax.ShapeDtypeStruct((local * slots, width), jnp.bfloat16)] * peers,
        compiler_params=pltpu.CompilerParams(vmem_limit_bytes=VMEM_LIMIT),
        cost_estimate=pl.CostEstimate(
            flops=2 * local * rows * width * inner,
            bytes_accessed=2 * local * (inner * width + rows * (inner + width)),
            transcendentals=0,
        ),
        name="expert_down",
    )(hidden, w_down)


def mix_kernel(order_ref, mix_ref, *refs, first, count):
    rows = jnp.concatenate([r[...] for r in refs[:-1]], axis=0)
    if count:
        span = refs[-1].shape[0] // count
        mix = jnp.concatenate(
            [
                mix_ref[pl.ds(pl.multiple_of(order_ref[first + i] * span, span), span), :]
                for i in range(count)
            ],
            axis=0,
        )
    else:
        mix = mix_ref[...]
    out = jnp.dot(mix, rows, preferred_element_type=jnp.float32)
    refs[-1][...] = out.astype(refs[-1].dtype)


def mix_rows(order, mix, parts, dtype, first=0, count=0, deps=()):
    rows = mix.shape[0] * (count or len(order)) // len(order)
    width = parts[0].shape[1]
    vmem = pl.BlockSpec(memory_space=pltpu.VMEM)
    return call(
        functools.partial(mix_kernel, first=first, count=count),
        deps,
        [order, mix, *parts],
        [pl.BlockSpec(memory_space=pltpu.SMEM)] + [vmem] * (1 + len(parts)),
        out_specs=vmem,
        out_shape=jax.ShapeDtypeStruct((rows, width), dtype),
        cost_estimate=pl.CostEstimate(
            flops=2 * rows * mix.shape[1] * width,
            bytes_accessed=2 * (mix.size + (mix.shape[0] + mix.shape[1]) * width),
            transcendentals=0,
        ),
        name="mix_rows",
    )


def table_kernel(order_ref, place_ref, gate_ref, pick_ref, mix_ref, *, slots):
    group, local, column = place_ref.shape
    blocks = order_ref.shape[0]
    span = column // blocks
    slot = lax.broadcasted_iota(jnp.int32, (slots, span), 0)
    for b in range(blocks):
        here = slice(b * span, (b + 1) * span)
        hits, gates = [], []
        for g in range(group):
            for j in range(local):
                hit = place_ref[g, j : j + 1, here] == slot
                hits.append(jnp.where(hit, 1.0, 0.0))
                gates.append(jnp.where(hit, gate_ref[g, j : j + 1, here], 0.0))
        at = pl.ds(pl.multiple_of(order_ref[b] * span, span), span)
        pick_ref[:, at] = jnp.concatenate(hits, axis=0).astype(pick_ref.dtype)
        mix_ref[at, :] = jnp.concatenate(gates, axis=0).T.astype(mix_ref.dtype)


def tables(order, place, gate, slots):
    peers, local, column = place.shape
    rows = local * slots
    group = next(g for g in range(1, peers + 1) if g == peers or not (peers % g or g * rows % 128))
    return pl.pallas_call(
        functools.partial(table_kernel, slots=slots),
        grid=(peers // group,),
        in_specs=[pl.BlockSpec(memory_space=pltpu.SMEM)]
        + [pl.BlockSpec((group, local, column), lambda k: (k, 0, 0))] * 2,
        out_specs=[
            pl.BlockSpec((group * rows, column), lambda k: (k, 0)),
            pl.BlockSpec((column, group * rows), lambda k: (0, k)),
        ],
        out_shape=[
            jax.ShapeDtypeStruct((peers * rows, column), jnp.bfloat16),
            jax.ShapeDtypeStruct((column, peers * rows), jnp.bfloat16),
        ],
        compiler_params=pltpu.CompilerParams(vmem_limit_bytes=VMEM_LIMIT),
        cost_estimate=pl.CostEstimate(
            flops=4 * peers * rows * column,
            bytes_accessed=4 * peers * rows * column,
            transcendentals=0,
        ),
        name="tables",
    )(order, place, gate)


def hold_kernel(x_ref, o_ref):
    o_ref[...] = x_ref[...]


def hold(value, deps):
    vmem = pl.BlockSpec(memory_space=pltpu.VMEM)
    return call(
        hold_kernel,
        deps,
        [value],
        [vmem],
        out_specs=vmem,
        out_shape=jax.ShapeDtypeStruct(value.shape, value.dtype),
        name="hold",
    )


def exchange(value, axis, k):
    if k == 0:
        return value
    return lax.ppermute(value, axis, [(i, i ^ k) for i in range(lax.axis_size(axis))])


def per_device(
    tokens,
    queries,
    keys_values,
    out_weight,
    moe_gain,
    expert_ids,
    gates,
    w_gate_experts,
    w_up_experts,
    w_down_experts,
):
    tok_count, width = tokens.shape
    ctx_count = lax.axis_size("ctx")
    peers = lax.axis_size("grp")
    chips = ctx_count // 2
    here, me = lax.axis_index("ctx"), lax.axis_index("grp")
    local = w_gate_experts.shape[0]
    slots = ctx_count * CAP
    column = ctx_count * tok_count
    turn = [k for k in reversed(range(peers))]

    order = here ^ jnp.concatenate(
        [2 * jnp.arange(chips, dtype=jnp.int32) + core for core in range(2)]
    )

    half = keys_values.shape[1] // 2
    kv_same = [exchange(keys_values[0, half:], "ctx", 2 * s) for s in reversed(range(chips))][::-1]
    kv_lead = lax.all_gather(keys_values[0, :half], "ctx", axis=0, tiled=True)
    kv_blocks = kv_same + [exchange(b, "ctx", 1) for b in kv_same]

    def route(attended):
        routes = jnp.concatenate([expert_ids.astype(jnp.float32), gates], axis=1).T
        routes = hold(routes, [attended])
        pair = jnp.concatenate([routes, exchange(routes, "ctx", 1)], axis=1)
        pairs = [exchange(pair, "ctx", 2 * s) for s in range(chips)]
        routes = jnp.concatenate(
            [p[:, :tok_count] for p in pairs] + [p[:, tok_count:] for p in pairs], axis=1
        )
        ids, gate_rows = routes[:TOPK].astype(jnp.int32), routes[TOPK:]
        owner = me ^ jnp.arange(peers, dtype=jnp.int32)
        wanted = (
            ((owner * ctx_count + here) * local)[:, None] + jnp.arange(local, dtype=jnp.int32)[None, :]
        ).reshape(-1)
        same = ids[None, :, :] == wanted[:, None, None]
        named = jnp.any(same, axis=1)
        gate_of = jnp.sum(jnp.where(same, gate_rows[None], 0.0), axis=1)
        earlier = jnp.triu(jnp.ones((tok_count, tok_count), jnp.bfloat16), 1)
        rank = jnp.dot(
            named.reshape(-1, tok_count).astype(jnp.bfloat16),
            earlier,
            preferred_element_type=jnp.float32,
        ).astype(jnp.int32)
        place = rank.reshape(-1, column) + jnp.repeat(order * CAP, tok_count)
        place = jnp.where(named, place, -1)
        pick, mix = tables(
            order, place.reshape(peers, local, column), gate_of.reshape(peers, local, column), slots
        )
        return pick, mix

    old = keys_values.shape[1] * ctx_count - column
    heads = H // peers
    sums, sent, deps = {}, {}, []
    for k in turn:
        peer = me ^ k
        where = jnp.concatenate(
            [
                jnp.stack([peer, peer * heads // (H // KV_HEADS), old + here * tok_count]).astype(
                    jnp.int32
                ),
                order,
            ]
        )
        if k == turn[0]:
            attended = attention(queries, kv_lead, kv_blocks, where, old, peers, deps)
            pick, mix = route(attended)
        if k == 0:
            for j in turn[:-1]:
                part = jnp.dot(sent[j], out_weight, preferred_element_type=jnp.float32)
                deps.append(part.astype(jnp.bfloat16))
                sums[j] = exchange(deps[-1], "grp", j)
            deps += [pick, mix]
        if k != turn[0]:
            attended = attention(queries, kv_lead, kv_blocks, where, old, peers, deps)
        sent[k] = exchange(attended, "grp", k)
    sums[0] = jnp.dot(sent[0], out_weight, preferred_element_type=jnp.float32)
    projected = sum(sums[k].astype(jnp.float32) for k in range(peers))
    residual = (tokens.astype(jnp.float32) + projected).astype(jnp.bfloat16)
    wide = residual.astype(jnp.float32)
    normed = (
        wide * lax.rsqrt(jnp.mean(wide * wide, axis=1, keepdims=True) + 1e-06) * moe_gain
    ).astype(jnp.bfloat16)

    span = width // CHUNKS
    same = [exchange(normed[:, :span], "ctx", 2 * s) for s in range(chips)]
    blocks = same + [exchange(jnp.concatenate(same, axis=0), "ctx", 1)]
    rest = lax.all_gather(normed[:, span:], "ctx", axis=0, tiled=True)
    rows = pick_rows(order, pick, blocks, peers)
    parts = []
    for c in range(CHUNKS):
        if c:
            rows = pick_rows(order, pick, [rest], peers, c - 1, CHUNKS - 1)
        sent = {k: exchange(rows[k], "grp", k) for k in turn}
        parts.append([sent[k] for k in range(peers)])
    carry, deps = None, [rows[0]]
    for c in range(CHUNKS):
        last = c == CHUNKS - 1
        carry = expert_hidden(
            parts[c], c * span, w_gate_experts, w_up_experts, carry, last, [] if last else deps
        )
    hidden = carry

    ready = [expert_down(hidden, w_down_experts, c, CHUNKS, peers) for c in range(CHUNKS)]
    early = CHUNKS // 2
    outs, totals = [], []
    for c in range(CHUNKS):
        sent = {k: exchange(ready[c][k], "grp", k) for k in turn}
        back = [sent[k] for k in range(peers)]
        if c < early:
            deps = [r[0] for r in ready[c + 1 :]]
            totals.append(mix_rows(order, mix, back, jnp.bfloat16, deps=deps))
            if c < early - 1:
                continue
            total = jnp.concatenate(totals, axis=1)
            total = lax.psum_scatter(total, "ctx", scatter_dimension=0, tiled=True)
            total = wide[:, : early * span] + total.astype(jnp.float32)
        else:
            other = mix_rows(order, mix, back, jnp.bfloat16, chips, chips, outs[1:])
            other = exchange(other, "ctx", 1)
            both = mix_rows(order, mix, back, jnp.float32, 0, chips) + other.astype(jnp.float32)
            total = wide[:, c * span : (c + 1) * span] + both[:tok_count]
            for s in range(1, chips):
                piece = both[s * tok_count : (s + 1) * tok_count].astype(jnp.bfloat16)
                total = total + exchange(piece, "ctx", 2 * s).astype(jnp.float32)
        outs.append(total.astype(jnp.bfloat16))
    return jnp.concatenate(outs, axis=1)


def solution(mesh):
    return jax.shard_map(
        per_device,
        mesh=mesh,
        in_specs=(
            P(("grp", "ctx"), None),
            P(("grp", "ctx"), None),
            P("grp", "ctx", None),
            P("grp", None),
            P(),
            P(("grp", "ctx"), None),
            P(("grp", "ctx"), None),
            P(("grp", "ctx"), None, None),
            P(("grp", "ctx"), None, None),
            P(("grp", "ctx"), None, None),
        ),
        out_specs=P(("grp", "ctx"), None),
        check_vma=False,
    )
```

```python
import functools
import math

import jax
import jax.numpy as jnp
from jax import lax
from jax.experimental import pallas as pl
from jax.experimental.pallas import tpu as pltpu
from jax.sharding import PartitionSpec as P

H = 32
KV_HEADS = 4
HEAD_DIM = 128
EXPERTS = 128
TOPK = 8
CAP = 12

CHUNKS = 4
VMEM_LIMIT = 48 * 1024 * 1024
VMEM_MOST = 60 * 1024 * 1024


def call(kernel, deps, operands, in_specs, vmem=VMEM_LIMIT, **kwargs):
    count = len(operands)

    def run(*refs):
        kernel(*refs[:count], *refs[count + len(deps) :])

    in_specs = in_specs + [pl.BlockSpec(memory_space=pl.ANY)] * len(deps)
    params = pltpu.CompilerParams(vmem_limit_bytes=vmem)
    if "grid_spec" in kwargs:
        kwargs["grid_spec"] = kwargs["grid_spec"](in_specs)
        in_specs = None
    else:
        kwargs["in_specs"] = in_specs
    return pl.pallas_call(run, compiler_params=params, **kwargs)(*operands, *deps)


def attention_kernel(where_ref, q_ref, *refs, blocks, stack, old):
    k_refs, v_refs = refs[: blocks + 1], refs[blocks + 1 : 2 * blocks + 2]
    o_ref, key_ref, value_ref = refs[2 * blocks + 2 :]
    rows, wide = q_ref.shape
    keys = key_ref.shape[0]
    span, lead = keys // blocks, k_refs[0].shape[0] // blocks
    factor = math.log2(math.e) / math.sqrt(HEAD_DIM)
    for b in range(blocks):
        at = slice(b * span, b * span + lead)
        part = slice(b * lead, (b + 1) * lead)
        key_ref[at, :] = k_refs[0][part, :]
        value_ref[at, :HEAD_DIM] = v_refs[0][part, :]
        at = pl.ds(pl.multiple_of(where_ref[3 + b] * span + lead, lead), span - lead)
        key_ref[at, :] = k_refs[1 + b][...]
        value_ref[at, :HEAD_DIM] = v_refs[1 + b][...]
    value_ref[:, HEAD_DIM:] = jnp.ones((keys, HEAD_DIM), value_ref.dtype)
    late = (stack * rows, keys - old)
    row = lax.broadcasted_iota(jnp.int32, late, 0) % rows
    allowed = lax.broadcasted_iota(jnp.int32, late, 1) + old <= row + where_ref[2]
    for first in range(0, wide // HEAD_DIM, stack):
        query = jnp.concatenate(
            [q_ref[:, h * HEAD_DIM : (h + 1) * HEAD_DIM] for h in range(first, first + stack)],
            axis=0,
        )
        scores = lax.dot_general(
            query, key_ref[...], (((1,), (1,)), ((), ())), preferred_element_type=jnp.float32
        )
        scores = jnp.concatenate(
            [scores[:, :old], jnp.where(allowed, scores[:, old:], -1e30)], axis=1
        )
        top = jnp.max(scores, axis=1, keepdims=True)
        weights = jnp.exp2((scores - top) * factor).astype(jnp.bfloat16)
        summed = jnp.dot(weights, value_ref[...], preferred_element_type=jnp.float32)
        out = (summed[:, :HEAD_DIM] / summed[:, HEAD_DIM:]).astype(o_ref.dtype)
        for i in range(stack):
            h = first + i
            o_ref[:, h * HEAD_DIM : (h + 1) * HEAD_DIM] = out[i * rows : (i + 1) * rows]


def attention(queries, kv_lead, kv_blocks, span, where, old, peers, deps):
    rows = queries.shape[0]
    wide = queries.shape[1] // peers
    blocks = len(kv_blocks)
    keys = blocks * span
    lead = kv_lead.shape[0] // blocks

    def column(size, first):
        return pl.BlockSpec((size, HEAD_DIM), lambda i, where: (0, first + where[1]))

    sizes = [lead * blocks] + [span - lead] * blocks
    return call(
        functools.partial(attention_kernel, blocks=blocks, stack=2, old=old),
        deps,
        [where, queries] + [kv_lead, *kv_blocks] * 2,
        [pl.BlockSpec((rows, wide), lambda i, where: (0, where[0]))]
        + [column(size, 0) for size in sizes]
        + [column(size, KV_HEADS) for size in sizes],
        grid_spec=lambda in_specs: pltpu.PrefetchScalarGridSpec(
            num_scalar_prefetch=1,
            grid=(1,),
            in_specs=in_specs,
            out_specs=pl.BlockSpec((rows, wide), lambda i, where: (0, 0)),
            scratch_shapes=[
                pltpu.VMEM((keys, HEAD_DIM), jnp.bfloat16),
                pltpu.VMEM((keys, 2 * HEAD_DIM), jnp.bfloat16),
            ],
        ),
        out_shape=jax.ShapeDtypeStruct((rows, wide), jnp.bfloat16),
        cost_estimate=pl.CostEstimate(
            flops=4 * rows * wide * keys,
            bytes_accessed=4 * (keys * HEAD_DIM + rows * wide),
            transcendentals=rows * wide // HEAD_DIM * keys,
        ),
        name="attention",
        vmem=VMEM_MOST,
    )


def pick_kernel(order_ref, pick_ref, *refs, blocks):
    if blocks > 1:
        block_refs, outs, scratch = refs[:blocks], refs[blocks:-1], refs[-1]
        span = block_refs[0].shape[0]
        number = 0
        for ref in block_refs:
            for part in range(ref.shape[0] // span):
                at = pl.ds(pl.multiple_of(order_ref[number] * span, span), span)
                scratch[at, :] = ref[part * span : (part + 1) * span, :]
                number += 1
        block = scratch[...]
    else:
        block, outs = refs[0][...], refs[1:]
    count = outs[0].shape[0]
    for k, out in enumerate(outs):
        out[...] = jnp.dot(
            pick_ref[k * count : (k + 1) * count, :], block, preferred_element_type=jnp.float32
        ).astype(out.dtype)


def pick_rows(order, pick, blocks, peers, chunk=0, chunks=1):
    count, width = pick.shape[0] // peers, blocks[0].shape[1] // chunks

    def whole(shape):
        return pl.BlockSpec(shape, lambda i: (0, 0))

    return call(
        functools.partial(pick_kernel, blocks=len(blocks)),
        [],
        [order, pick, *blocks],
        [pl.BlockSpec(memory_space=pltpu.SMEM), whole(pick.shape)]
        + [pl.BlockSpec((b.shape[0], width), lambda i: (0, chunk)) for b in blocks],
        grid=(1,),
        out_specs=[whole((count, width))] * peers,
        out_shape=[jax.ShapeDtypeStruct((count, width), jnp.bfloat16)] * peers,
        scratch_shapes=[pltpu.VMEM((pick.shape[1], width), jnp.bfloat16)] * (len(blocks) > 1),
        cost_estimate=pl.CostEstimate(
            flops=2 * pick.size * width,
            bytes_accessed=2 * (pick.size + (pick.shape[0] + pick.shape[1]) * width),
            transcendentals=0,
        ),
        name="pick_rows",
    )


def hidden_kernel(*refs, peers, carried, last):
    x_refs, refs = refs[:peers], refs[peers:]
    gate_ref, up_ref, *refs = refs
    part = jnp.concatenate([x[...] for x in x_refs], axis=0)
    gate = jnp.dot(part, gate_ref[0], preferred_element_type=jnp.float32)
    up = jnp.dot(part, up_ref[0], preferred_element_type=jnp.float32)
    if carried:
        gate = gate + refs[0][0]
        up = up + refs[1][0]
        refs = refs[2:]
    if last:
        refs[0][0] = (gate / (1.0 + jnp.exp(-gate)) * up).astype(refs[0].dtype)
    else:
        refs[0][0] = gate
        refs[1][0] = up


def expert_hidden(part, first, w_gate, w_up, carry, last, deps=()):
    peers = len(part)
    width = part[0].shape[1]
    local, _, inner = w_gate.shape
    slots = part[0].shape[0] // local
    rows = peers * slots
    assert first % width == 0
    weight_spec = pl.BlockSpec((1, width, inner), lambda j: (j, first // width, 0))
    sum_spec = pl.BlockSpec((1, rows, inner), lambda j: (j, 0, 0))
    total = jax.ShapeDtypeStruct((local, rows, inner), jnp.float32)
    return call(
        functools.partial(hidden_kernel, peers=peers, carried=carry is not None, last=last),
        deps,
        [*part, w_gate, w_up, *(carry or ())],
        [pl.BlockSpec((slots, width), lambda j: (j, 0))] * peers
        + [weight_spec] * 2
        + ([] if carry is None else [sum_spec] * 2),
        grid=(local,),
        out_specs=sum_spec if last else [sum_spec] * 2,
        out_shape=jax.ShapeDtypeStruct(total.shape, jnp.bfloat16) if last else [total] * 2,
        cost_estimate=pl.CostEstimate(
            flops=4 * local * rows * width * inner,
            bytes_accessed=4 * local * width * inner + 10 * local * rows * inner,
            transcendentals=local * rows * inner,
        ),
        name="expert_hidden",
    )


def down_kernel(h_ref, w_ref, *y_refs):
    slots = y_refs[0].shape[0]
    out = jnp.dot(h_ref[0], w_ref[0], preferred_element_type=jnp.float32).astype(jnp.bfloat16)
    for k, y_ref in enumerate(y_refs):
        y_ref[...] = out[k * slots : (k + 1) * slots]


def expert_down(hidden, w_down, chunk, chunks, peers):
    local, rows, inner = hidden.shape
    width = w_down.shape[2] // chunks
    slots = rows // peers
    return pl.pallas_call(
        down_kernel,
        grid=(local,),
        in_specs=[
            pl.BlockSpec((1, rows, inner), lambda j: (j, 0, 0)),
            pl.BlockSpec((1, inner, width), lambda j: (j, 0, chunk)),
        ],
        out_specs=[pl.BlockSpec((slots, width), lambda j: (j, 0))] * peers,
        out_shape=[jax.ShapeDtypeStruct((local * slots, width), jnp.bfloat16)] * peers,
        compiler_params=pltpu.CompilerParams(vmem_limit_bytes=VMEM_LIMIT),
        cost_estimate=pl.CostEstimate(
            flops=2 * local * rows * width * inner,
            bytes_accessed=2 * local * (inner * width + rows * (inner + width)),
            transcendentals=0,
        ),
        name="expert_down",
    )(hidden, w_down)


def mix_kernel(order_ref, mix_ref, *refs, first, count):
    rows = jnp.concatenate([r[...] for r in refs[:-1]], axis=0)
    if count:
        span = refs[-1].shape[0] // count
        mix = jnp.concatenate(
            [
                mix_ref[pl.ds(pl.multiple_of(order_ref[first + i] * span, span), span), :]
                for i in range(count)
            ],
            axis=0,
        )
    else:
        mix = mix_ref[...]
    out = jnp.dot(mix, rows, preferred_element_type=jnp.float32)
    refs[-1][...] = out.astype(refs[-1].dtype)


def mix_rows(order, mix, parts, dtype, first=0, count=0, deps=()):
    rows = mix.shape[0] * (count or len(order)) // len(order)
    width = parts[0].shape[1]
    vmem = pl.BlockSpec(memory_space=pltpu.VMEM)
    return call(
        functools.partial(mix_kernel, first=first, count=count),
        deps,
        [order, mix, *parts],
        [pl.BlockSpec(memory_space=pltpu.SMEM)] + [vmem] * (1 + len(parts)),
        out_specs=vmem,
        out_shape=jax.ShapeDtypeStruct((rows, width), dtype),
        cost_estimate=pl.CostEstimate(
            flops=2 * rows * mix.shape[1] * width,
            bytes_accessed=2 * (mix.size + (mix.shape[0] + mix.shape[1]) * width),
            transcendentals=0,
        ),
        name="mix_rows",
    )


def table_kernel(order_ref, place_ref, gate_ref, pick_ref, mix_ref, *, slots):
    group, local, column = place_ref.shape
    blocks = order_ref.shape[0]
    span = column // blocks
    slot = lax.broadcasted_iota(jnp.int32, (slots, span), 0)
    for b in range(blocks):
        here = slice(b * span, (b + 1) * span)
        hits, gates = [], []
        for g in range(group):
            for j in range(local):
                hit = place_ref[g, j : j + 1, here] == slot
                hits.append(jnp.where(hit, 1.0, 0.0))
                gates.append(jnp.where(hit, gate_ref[g, j : j + 1, here], 0.0))
        at = pl.ds(pl.multiple_of(order_ref[b] * span, span), span)
        pick_ref[:, at] = jnp.concatenate(hits, axis=0).astype(pick_ref.dtype)
        mix_ref[at, :] = jnp.concatenate(gates, axis=0).T.astype(mix_ref.dtype)


def tables(order, place, gate, slots):
    peers, local, column = place.shape
    rows = local * slots
    group = next(g for g in range(1, peers + 1) if g == peers or not (peers % g or g * rows % 128))
    return pl.pallas_call(
        functools.partial(table_kernel, slots=slots),
        grid=(peers // group,),
        in_specs=[pl.BlockSpec(memory_space=pltpu.SMEM)]
        + [pl.BlockSpec((group, local, column), lambda k: (k, 0, 0))] * 2,
        out_specs=[
            pl.BlockSpec((group * rows, column), lambda k: (k, 0)),
            pl.BlockSpec((column, group * rows), lambda k: (0, k)),
        ],
        out_shape=[
            jax.ShapeDtypeStruct((peers * rows, column), jnp.bfloat16),
            jax.ShapeDtypeStruct((column, peers * rows), jnp.bfloat16),
        ],
        compiler_params=pltpu.CompilerParams(vmem_limit_bytes=VMEM_LIMIT),
        cost_estimate=pl.CostEstimate(
            flops=4 * peers * rows * column,
            bytes_accessed=4 * peers * rows * column,
            transcendentals=0,
        ),
        name="tables",
    )(order, place, gate)


def norm_kernel(tokens_ref, own_ref, gain_ref, *refs):
    *part_refs, res_ref, first_ref, rest_ref = refs
    width, span = tokens_ref.shape[1], first_ref.shape[1]
    total = own_ref[...]
    for ref in part_refs:
        total = total + ref[...].astype(jnp.float32)
    res = (tokens_ref[...].astype(jnp.float32) + total).astype(res_ref.dtype)
    res_ref[...] = res
    res = res.astype(jnp.float32)
    mean = jnp.sum(res * res, axis=1, keepdims=True) * (1.0 / width)
    normed = (res * lax.rsqrt(mean + 1e-06) * gain_ref[...]).astype(first_ref.dtype)
    first_ref[...] = normed[:, :span]
    rest_ref[...] = normed[:, span:]


def norm(tokens, own, gain, parts, span):
    rows, width = tokens.shape
    vmem = pl.BlockSpec(memory_space=pltpu.VMEM)
    operands = [tokens, own, gain, *parts]
    return call(
        norm_kernel,
        [],
        operands,
        [vmem] * len(operands),
        out_specs=[vmem] * 3,
        out_shape=[
            jax.ShapeDtypeStruct((rows, size), jnp.bfloat16) for size in (width, span, width - span)
        ],
        name="norm",
    )


def exchange(value, axis, k):
    if k == 0:
        return value
    return lax.ppermute(value, axis, [(i, i ^ k) for i in range(lax.axis_size(axis))])


def chip_exchange(value, turn):
    if turn == 0:
        return value
    count = lax.axis_size("ctx")
    steps = (2 * turn, count - 2 * turn)
    return lax.ppermute(value, "ctx", [(i, i ^ steps[i % 2]) for i in range(count)])


def per_device(
    tokens,
    queries,
    keys_values,
    out_weight,
    moe_gain,
    expert_ids,
    gates,
    w_gate_experts,
    w_up_experts,
    w_down_experts,
):
    tok_count, width = tokens.shape
    ctx_count = lax.axis_size("ctx")
    peers = lax.axis_size("grp")
    chips = ctx_count // 2
    here, me = lax.axis_index("ctx"), lax.axis_index("grp")
    local = w_gate_experts.shape[0]
    slots = ctx_count * CAP
    column = ctx_count * tok_count
    turn = [k for k in reversed(range(peers))]

    turns = 2 * jnp.arange(chips, dtype=jnp.int32)
    back_turns = (ctx_count - turns) % ctx_count
    even = here % 2 == 0
    order = here ^ jnp.concatenate(
        [
            jnp.where(even, turns, back_turns),
            jnp.where(even, back_turns, turns) + 1,
        ]
    )

    kv_span = keys_values.shape[1]
    lead = kv_span // 2
    routes = jnp.concatenate([expert_ids.astype(jnp.bfloat16), gates.astype(jnp.bfloat16)], axis=1)
    routes = jnp.pad(routes.T, ((0, 0), (0, keys_values.shape[2] - tok_count)))
    block = jnp.concatenate([keys_values[0, lead:], routes], axis=0)
    kv_same = [chip_exchange(block, s) for s in reversed(range(chips))][::-1]
    kv_lead = lax.all_gather(keys_values[0, :lead], "ctx", axis=0, tiled=True)
    kv_blocks = kv_same + [exchange(b, "ctx", 1) for b in kv_same]

    routes = jnp.concatenate([b[kv_span - lead :, :tok_count] for b in kv_blocks], axis=1).astype(jnp.float32)
    ids, gate_rows = routes[:TOPK].astype(jnp.int32), routes[TOPK:]
    owner = me ^ jnp.arange(peers, dtype=jnp.int32)
    wanted = (
        ((owner * ctx_count + here) * local)[:, None] + jnp.arange(local, dtype=jnp.int32)[None, :]
    ).reshape(-1)
    same = ids[None, :, :] == wanted[:, None, None]
    named = jnp.any(same, axis=1)
    gate_of = jnp.sum(jnp.where(same, gate_rows[None], 0.0), axis=1)
    earlier = jnp.triu(jnp.ones((tok_count, tok_count), jnp.bfloat16), 1)
    rank = jnp.dot(
        named.reshape(-1, tok_count).astype(jnp.bfloat16),
        earlier,
        preferred_element_type=jnp.float32,
    ).astype(jnp.int32)
    place = rank.reshape(-1, column) + jnp.repeat(order * CAP, tok_count)
    place = jnp.where(named, place, -1)
    pick, mix = tables(
        order, place.reshape(peers, local, column), gate_of.reshape(peers, local, column), slots
    )

    old = keys_values.shape[1] * ctx_count - column
    heads = H // peers
    sent, deps = {}, []
    for k in turn:
        peer = me ^ k
        where = jnp.concatenate(
            [
                jnp.stack([peer, peer * heads // (H // KV_HEADS), old + here * tok_count]).astype(
                    jnp.int32
                ),
                order,
            ]
        )
        if k == 0:
            deps = [
                jnp.dot(sent[j], out_weight, preferred_element_type=jnp.float32).astype(jnp.bfloat16)
                for j in turn[:-1]
            ]
            sums = [exchange(d, "grp", j) for j, d in zip(turn[:-1], deps)]
            deps = deps + [pick, mix]
        attended = attention(queries, kv_lead, kv_blocks, kv_span, where, old, peers, deps)
        sent[k] = exchange(attended, "grp", k)
    own = jnp.dot(sent[0], out_weight, preferred_element_type=jnp.float32)
    span = width // CHUNKS
    residual, first, rest = norm(tokens, own, moe_gain[None, :], sums, span)
    wide = residual.astype(jnp.float32)

    same = [chip_exchange(first, s) for s in range(chips)]
    blocks = same + [exchange(jnp.concatenate(same, axis=0), "ctx", 1)]
    rest = lax.all_gather(rest, "ctx", axis=0, tiled=True)
    rows = pick_rows(order, pick, blocks, peers)
    parts = []
    for c in range(CHUNKS):
        if c:
            rows = pick_rows(order, pick, [rest], peers, c - 1, CHUNKS - 1)
        sent = {k: exchange(rows[k], "grp", k) for k in turn}
        parts.append([sent[k] for k in range(peers)])
    carry, deps = None, [rows[0]]
    for c in range(CHUNKS):
        last = c == CHUNKS - 1
        carry = expert_hidden(
            parts[c], c * span, w_gate_experts, w_up_experts, carry, last, [] if last else deps
        )
    hidden = carry

    ready = [expert_down(hidden, w_down_experts, c, CHUNKS, peers) for c in range(CHUNKS)]
    early = CHUNKS // 2
    outs, totals = [], []
    for c in range(CHUNKS):
        sent = {k: exchange(ready[c][k], "grp", k) for k in turn}
        back = [sent[k] for k in range(peers)]
        if c < early:
            deps = [r[0] for r in ready[c + 1 :]]
            totals.append(mix_rows(order, mix, back, jnp.bfloat16, deps=deps))
            if c < early - 1:
                continue
            total = jnp.concatenate(totals, axis=1)
            total = lax.psum_scatter(total, "ctx", scatter_dimension=0, tiled=True)
            total = wide[:, : early * span] + total.astype(jnp.float32)
        else:
            other = mix_rows(order, mix, back, jnp.bfloat16, chips, chips, outs[1:])
            other = exchange(other, "ctx", 1)
            both = mix_rows(order, mix, back, jnp.float32, 0, chips) + other.astype(jnp.float32)
            total = wide[:, c * span : (c + 1) * span] + both[:tok_count]
            for s in range(1, chips):
                piece = both[s * tok_count : (s + 1) * tok_count].astype(jnp.bfloat16)
                total = total + chip_exchange(piece, s).astype(jnp.float32)
        outs.append(total.astype(jnp.bfloat16))
    return jnp.concatenate(outs, axis=1)


def solution(mesh):
    return jax.shard_map(
        per_device,
        mesh=mesh,
        in_specs=(
            P(("grp", "ctx"), None),
            P(("grp", "ctx"), None),
            P("grp", "ctx", None),
            P("grp", None),
            P(),
            P(("grp", "ctx"), None),
            P(("grp", "ctx"), None),
            P(("grp", "ctx"), None, None),
            P(("grp", "ctx"), None, None),
            P(("grp", "ctx"), None, None),
        ),
        out_specs=P(("grp", "ctx"), None),
        check_vma=False,
    )
```

```python
import functools
import math

import jax
import jax.numpy as jnp
from jax import lax
from jax.experimental import pallas as pl
from jax.experimental.pallas import tpu as pltpu
from jax.sharding import PartitionSpec as P

H = 32
KV_HEADS = 4
HEAD_DIM = 128
EXPERTS = 128
TOPK = 8
CAP = 12

CHUNKS = 4
VMEM_LIMIT = 24 * 1024 * 1024
VMEM_MOST = 60 * 1024 * 1024


def call(kernel, deps, operands, in_specs, vmem=VMEM_LIMIT, **kwargs):
    count = len(operands)

    def run(*refs):
        kernel(*refs[:count], *refs[count + len(deps) :])

    in_specs = in_specs + [pl.BlockSpec(memory_space=pl.ANY)] * len(deps)
    params = pltpu.CompilerParams(vmem_limit_bytes=vmem)
    if "grid_spec" in kwargs:
        kwargs["grid_spec"] = kwargs["grid_spec"](in_specs)
        in_specs = None
    else:
        kwargs["in_specs"] = in_specs
    return pl.pallas_call(run, compiler_params=params, **kwargs)(*operands, *deps)


def attention_kernel(where_ref, q_ref, *refs, blocks, stack, old):
    k_refs, v_refs = refs[: blocks + 1], refs[blocks + 1 : 2 * blocks + 2]
    o_ref, key_ref, value_ref = refs[2 * blocks + 2 :]
    rows, wide = q_ref.shape
    keys = key_ref.shape[0]
    span, lead = keys // blocks, k_refs[0].shape[0] // blocks
    factor = math.log2(math.e) / math.sqrt(HEAD_DIM)
    for b in range(blocks):
        at = slice(b * span, b * span + lead)
        part = slice(b * lead, (b + 1) * lead)
        key_ref[at, :] = k_refs[0][part, :]
        value_ref[at, :HEAD_DIM] = v_refs[0][part, :]
        at = pl.ds(pl.multiple_of(where_ref[3 + b] * span + lead, lead), span - lead)
        key_ref[at, :] = k_refs[1 + b][...]
        value_ref[at, :HEAD_DIM] = v_refs[1 + b][...]
    value_ref[:, HEAD_DIM:] = jnp.ones((keys, HEAD_DIM), value_ref.dtype)
    late = (stack * rows, keys - old)
    row = lax.broadcasted_iota(jnp.int32, late, 0) % rows
    allowed = lax.broadcasted_iota(jnp.int32, late, 1) + old <= row + where_ref[2]
    for first in range(0, wide // HEAD_DIM, stack):
        query = jnp.concatenate(
            [q_ref[:, h * HEAD_DIM : (h + 1) * HEAD_DIM] for h in range(first, first + stack)],
            axis=0,
        )
        scores = lax.dot_general(
            query, key_ref[...], (((1,), (1,)), ((), ())), preferred_element_type=jnp.float32
        )
        scores = jnp.concatenate(
            [scores[:, :old], jnp.where(allowed, scores[:, old:], -1e30)], axis=1
        )
        top = jnp.max(scores, axis=1, keepdims=True)
        weights = jnp.exp2((scores - top) * factor).astype(jnp.bfloat16)
        summed = jnp.dot(weights, value_ref[...], preferred_element_type=jnp.float32)
        out = (summed[:, :HEAD_DIM] / summed[:, HEAD_DIM:]).astype(o_ref.dtype)
        for i in range(stack):
            h = first + i
            o_ref[:, h * HEAD_DIM : (h + 1) * HEAD_DIM] = out[i * rows : (i + 1) * rows]


def attention(queries, kv_lead, kv_blocks, span, where, old, peers, deps):
    rows = queries.shape[0]
    wide = queries.shape[1] // peers
    blocks = len(kv_blocks)
    keys = blocks * span
    lead = kv_lead.shape[0] // blocks

    def column(size, first):
        return pl.BlockSpec((size, HEAD_DIM), lambda i, where: (0, first + where[1]))

    sizes = [lead * blocks] + [span - lead] * blocks
    return call(
        functools.partial(attention_kernel, blocks=blocks, stack=2, old=old),
        deps,
        [where, queries] + [kv_lead, *kv_blocks] * 2,
        [pl.BlockSpec((rows, wide), lambda i, where: (0, where[0]))]
        + [column(size, 0) for size in sizes]
        + [column(size, KV_HEADS) for size in sizes],
        grid_spec=lambda in_specs: pltpu.PrefetchScalarGridSpec(
            num_scalar_prefetch=1,
            grid=(1,),
            in_specs=in_specs,
            out_specs=pl.BlockSpec((rows, wide), lambda i, where: (0, 0)),
            scratch_shapes=[
                pltpu.VMEM((keys, HEAD_DIM), jnp.bfloat16),
                pltpu.VMEM((keys, 2 * HEAD_DIM), jnp.bfloat16),
            ],
        ),
        out_shape=jax.ShapeDtypeStruct((rows, wide), jnp.bfloat16),
        cost_estimate=pl.CostEstimate(
            flops=4 * rows * wide * keys,
            bytes_accessed=4 * (keys * HEAD_DIM + rows * wide),
            transcendentals=rows * wide // HEAD_DIM * keys,
        ),
        name="attention",
        vmem=51 * 1024 * 1024,
    )


def pick_kernel(order_ref, pick_ref, *refs, blocks):
    if blocks > 1:
        block_refs, outs, scratch = refs[:blocks], refs[blocks:-1], refs[-1]
        span = block_refs[0].shape[0]
        number = 0
        for ref in block_refs:
            for part in range(ref.shape[0] // span):
                at = pl.ds(pl.multiple_of(order_ref[number] * span, span), span)
                scratch[at, :] = ref[part * span : (part + 1) * span, :]
                number += 1
        block = scratch[...]
    else:
        block, outs = refs[0][...], refs[1:]
    count = outs[0].shape[0]
    for k, out in enumerate(outs):
        out[...] = jnp.dot(
            pick_ref[k * count : (k + 1) * count, :], block, preferred_element_type=jnp.float32
        ).astype(out.dtype)


def pick_rows(order, pick, blocks, peers, chunk=0, chunks=1):
    count, width = pick.shape[0] // peers, blocks[0].shape[1] // chunks

    def whole(shape):
        return pl.BlockSpec(shape, lambda i: (0, 0))

    return call(
        functools.partial(pick_kernel, blocks=len(blocks)),
        [],
        [order, pick, *blocks],
        [pl.BlockSpec(memory_space=pltpu.SMEM), whole(pick.shape)]
        + [pl.BlockSpec((b.shape[0], width), lambda i: (0, chunk)) for b in blocks],
        grid=(1,),
        out_specs=[whole((count, width))] * peers,
        out_shape=[jax.ShapeDtypeStruct((count, width), jnp.bfloat16)] * peers,
        scratch_shapes=[pltpu.VMEM((pick.shape[1], width), jnp.bfloat16)] * (len(blocks) > 1),
        cost_estimate=pl.CostEstimate(
            flops=2 * pick.size * width,
            bytes_accessed=2 * (pick.size + (pick.shape[0] + pick.shape[1]) * width),
            transcendentals=0,
        ),
        name="pick_rows",
        vmem=48 * 1024 * 1024,
    )


def hidden_kernel(*refs, peers, carried, last):
    x_refs, refs = refs[:peers], refs[peers:]
    gate_ref, up_ref, *refs = refs
    part = jnp.concatenate([x[...] for x in x_refs], axis=0)
    gate = jnp.dot(part, gate_ref[0], preferred_element_type=jnp.float32)
    up = jnp.dot(part, up_ref[0], preferred_element_type=jnp.float32)
    if carried:
        gate = gate + refs[0][0]
        up = up + refs[1][0]
        refs = refs[2:]
    if last:
        refs[0][0] = (gate / (1.0 + jnp.exp(-gate)) * up).astype(refs[0].dtype)
    else:
        refs[0][0] = gate
        refs[1][0] = up


def expert_hidden(part, first, w_gate, w_up, carry, last, deps=()):
    peers = len(part)
    width = part[0].shape[1]
    local, _, inner = w_gate.shape
    slots = part[0].shape[0] // local
    rows = peers * slots
    assert first % width == 0
    weight_spec = pl.BlockSpec((1, width, inner), lambda j: (j, first // width, 0))
    sum_spec = pl.BlockSpec((1, rows, inner), lambda j: (j, 0, 0))
    total = jax.ShapeDtypeStruct((local, rows, inner), jnp.float32)
    return call(
        functools.partial(hidden_kernel, peers=peers, carried=carry is not None, last=last),
        deps,
        [*part, w_gate, w_up, *(carry or ())],
        [pl.BlockSpec((slots, width), lambda j: (j, 0))] * peers
        + [weight_spec] * 2
        + ([] if carry is None else [sum_spec] * 2),
        grid=(local,),
        out_specs=sum_spec if last else [sum_spec] * 2,
        out_shape=jax.ShapeDtypeStruct(total.shape, jnp.bfloat16) if last else [total] * 2,
        cost_estimate=pl.CostEstimate(
            flops=4 * local * rows * width * inner,
            bytes_accessed=4 * local * width * inner + 10 * local * rows * inner,
            transcendentals=local * rows * inner,
        ),
        name="expert_hidden",
        vmem=24 * 1024 * 1024,
    )


def down_kernel(h_ref, w_ref, *y_refs):
    slots = y_refs[0].shape[0]
    out = jnp.dot(h_ref[0], w_ref[0], preferred_element_type=jnp.float32).astype(jnp.bfloat16)
    for k, y_ref in enumerate(y_refs):
        y_ref[...] = out[k * slots : (k + 1) * slots]


def expert_down(hidden, w_down, chunk, chunks, peers):
    local, rows, inner = hidden.shape
    width = w_down.shape[2] // chunks
    slots = rows // peers
    return pl.pallas_call(
        down_kernel,
        grid=(local,),
        in_specs=[
            pl.BlockSpec((1, rows, inner), lambda j: (j, 0, 0)),
            pl.BlockSpec((1, inner, width), lambda j: (j, 0, chunk)),
        ],
        out_specs=[pl.BlockSpec((slots, width), lambda j: (j, 0))] * peers,
        out_shape=[jax.ShapeDtypeStruct((local * slots, width), jnp.bfloat16)] * peers,
        compiler_params=pltpu.CompilerParams(vmem_limit_bytes=48 * 1024 * 1024),
        cost_estimate=pl.CostEstimate(
            flops=2 * local * rows * width * inner,
            bytes_accessed=2 * local * (inner * width + rows * (inner + width)),
            transcendentals=0,
        ),
        name="expert_down",
    )(hidden, w_down)


def mix_kernel(order_ref, mix_ref, *refs, first, count):
    rows = jnp.concatenate([r[...] for r in refs[:-1]], axis=0)
    if count:
        span = refs[-1].shape[0] // count
        mix = jnp.concatenate(
            [
                mix_ref[pl.ds(pl.multiple_of(order_ref[first + i] * span, span), span), :]
                for i in range(count)
            ],
            axis=0,
        )
    else:
        mix = mix_ref[...]
    out = jnp.dot(mix, rows, preferred_element_type=jnp.float32)
    refs[-1][...] = out.astype(refs[-1].dtype)


def mix_rows(order, mix, parts, dtype, first=0, count=0, deps=()):
    rows = mix.shape[0] * (count or len(order)) // len(order)
    width = parts[0].shape[1]
    vmem = pl.BlockSpec(memory_space=pltpu.VMEM)
    return call(
        functools.partial(mix_kernel, first=first, count=count),
        deps,
        [order, mix, *parts],
        [pl.BlockSpec(memory_space=pltpu.SMEM)] + [vmem] * (1 + len(parts)),
        out_specs=vmem,
        out_shape=jax.ShapeDtypeStruct((rows, width), dtype),
        cost_estimate=pl.CostEstimate(
            flops=2 * rows * mix.shape[1] * width,
            bytes_accessed=2 * (mix.size + (mix.shape[0] + mix.shape[1]) * width),
            transcendentals=0,
        ),
        name="mix_rows",
        vmem=48 * 1024 * 1024,
    )


def table_kernel(order_ref, place_ref, gate_ref, pick_ref, mix_ref, *, slots):
    group, local, column = place_ref.shape
    blocks = order_ref.shape[0]
    span = column // blocks
    slot = lax.broadcasted_iota(jnp.int32, (slots, span), 0)
    for b in range(blocks):
        here = slice(b * span, (b + 1) * span)
        hits, gates = [], []
        for g in range(group):
            for j in range(local):
                hit = place_ref[g, j : j + 1, here] == slot
                hits.append(jnp.where(hit, 1.0, 0.0))
                gates.append(jnp.where(hit, gate_ref[g, j : j + 1, here], 0.0))
        at = pl.ds(pl.multiple_of(order_ref[b] * span, span), span)
        pick_ref[:, at] = jnp.concatenate(hits, axis=0).astype(pick_ref.dtype)
        mix_ref[at, :] = jnp.concatenate(gates, axis=0).T.astype(mix_ref.dtype)


def tables(order, place, gate, slots):
    peers, local, column = place.shape
    rows = local * slots
    group = next(g for g in range(1, peers + 1) if g == peers or not (peers % g or g * rows % 128))
    return pl.pallas_call(
        functools.partial(table_kernel, slots=slots),
        grid=(peers // group,),
        in_specs=[pl.BlockSpec(memory_space=pltpu.SMEM)]
        + [pl.BlockSpec((group, local, column), lambda k: (k, 0, 0))] * 2,
        out_specs=[
            pl.BlockSpec((group * rows, column), lambda k: (k, 0)),
            pl.BlockSpec((column, group * rows), lambda k: (0, k)),
        ],
        out_shape=[
            jax.ShapeDtypeStruct((peers * rows, column), jnp.bfloat16),
            jax.ShapeDtypeStruct((column, peers * rows), jnp.bfloat16),
        ],
        compiler_params=pltpu.CompilerParams(vmem_limit_bytes=48 * 1024 * 1024),
        cost_estimate=pl.CostEstimate(
            flops=4 * peers * rows * column,
            bytes_accessed=4 * peers * rows * column,
            transcendentals=0,
        ),
        name="tables",
    )(order, place, gate)


def norm_kernel(tokens_ref, own_ref, gain_ref, *refs):
    *part_refs, res_ref, first_ref, rest_ref = refs
    width, span = tokens_ref.shape[1], first_ref.shape[1]
    total = own_ref[...]
    for ref in part_refs:
        total = total + ref[...].astype(jnp.float32)
    res = (tokens_ref[...].astype(jnp.float32) + total).astype(res_ref.dtype)
    res_ref[...] = res
    res = res.astype(jnp.float32)
    mean = jnp.sum(res * res, axis=1, keepdims=True) * (1.0 / width)
    normed = (res * lax.rsqrt(mean + 1e-06) * gain_ref[...]).astype(first_ref.dtype)
    first_ref[...] = normed[:, :span]
    rest_ref[...] = normed[:, span:]


def norm(tokens, own, gain, parts, span):
    rows, width = tokens.shape
    vmem = pl.BlockSpec(memory_space=pltpu.VMEM)
    operands = [tokens, own, gain, *parts]
    return call(
        norm_kernel,
        [],
        operands,
        [vmem] * len(operands),
        out_specs=[vmem] * 3,
        out_shape=[
            jax.ShapeDtypeStruct((rows, size), jnp.bfloat16) for size in (width, span, width - span)
        ],
        name="norm",
    )


def exchange(value, axis, k):
    if k == 0:
        return value
    return lax.ppermute(value, axis, [(i, i ^ k) for i in range(lax.axis_size(axis))])


def chip_exchange(value, turn):
    if turn == 0:
        return value
    count = lax.axis_size("ctx")
    steps = (2 * turn, count - 2 * turn)
    return lax.ppermute(value, "ctx", [(i, i ^ steps[i % 2]) for i in range(count)])


def per_device(
    tokens,
    queries,
    keys_values,
    out_weight,
    moe_gain,
    expert_ids,
    gates,
    w_gate_experts,
    w_up_experts,
    w_down_experts,
):
    tok_count, width = tokens.shape
    ctx_count = lax.axis_size("ctx")
    peers = lax.axis_size("grp")
    chips = ctx_count // 2
    here, me = lax.axis_index("ctx"), lax.axis_index("grp")
    local = w_gate_experts.shape[0]
    slots = ctx_count * CAP
    column = ctx_count * tok_count
    turn = [k for k in reversed(range(peers))]

    turns = 2 * jnp.arange(chips, dtype=jnp.int32)
    back_turns = (ctx_count - turns) % ctx_count
    even = here % 2 == 0
    order = here ^ jnp.concatenate(
        [
            jnp.where(even, turns, back_turns),
            jnp.where(even, back_turns, turns) + 1,
        ]
    )

    kv_span = keys_values.shape[1]
    lead = kv_span // 2
    routes = jnp.concatenate([expert_ids.astype(jnp.bfloat16), gates.astype(jnp.bfloat16)], axis=1)
    routes = jnp.pad(routes.T, ((0, 0), (0, keys_values.shape[2] - tok_count)))
    block = jnp.concatenate([keys_values[0, lead:], routes], axis=0)
    kv_same = [chip_exchange(block, s) for s in reversed(range(chips))][::-1]
    kv_lead = lax.all_gather(keys_values[0, :lead], "ctx", axis=0, tiled=True)
    kv_blocks = kv_same + [exchange(b, "ctx", 1) for b in kv_same]

    routes = jnp.concatenate([b[kv_span - lead :, :tok_count] for b in kv_blocks], axis=1).astype(jnp.float32)
    ids, gate_rows = routes[:TOPK].astype(jnp.int32), routes[TOPK:]
    owner = me ^ jnp.arange(peers, dtype=jnp.int32)
    wanted = (
        ((owner * ctx_count + here) * local)[:, None] + jnp.arange(local, dtype=jnp.int32)[None, :]
    ).reshape(-1)
    same = ids[None, :, :] == wanted[:, None, None]
    named = jnp.any(same, axis=1)
    gate_of = jnp.sum(jnp.where(same, gate_rows[None], 0.0), axis=1)
    earlier = jnp.triu(jnp.ones((tok_count, tok_count), jnp.bfloat16), 1)
    rank = jnp.dot(
        named.reshape(-1, tok_count).astype(jnp.bfloat16),
        earlier,
        preferred_element_type=jnp.float32,
    ).astype(jnp.int32)
    place = rank.reshape(-1, column) + jnp.repeat(order * CAP, tok_count)
    place = jnp.where(named, place, -1)
    pick, mix = tables(
        order, place.reshape(peers, local, column), gate_of.reshape(peers, local, column), slots
    )

    old = keys_values.shape[1] * ctx_count - column
    heads = H // peers
    sent, deps = {}, []
    for k in turn:
        peer = me ^ k
        where = jnp.concatenate(
            [
                jnp.stack([peer, peer * heads // (H // KV_HEADS), old + here * tok_count]).astype(
                    jnp.int32
                ),
                order,
            ]
        )
        if k == 0:
            deps = [
                jnp.dot(sent[j], out_weight, preferred_element_type=jnp.float32).astype(jnp.bfloat16)
                for j in turn[:-1]
            ]
            sums = [exchange(d, "grp", j) for j, d in zip(turn[:-1], deps)]
            deps = deps + [pick, mix]
        attended = attention(queries, kv_lead, kv_blocks, kv_span, where, old, peers, deps)
        sent[k] = exchange(attended, "grp", k)
    own = jnp.dot(sent[0], out_weight, preferred_element_type=jnp.float32)
    span = width // CHUNKS
    residual, first, rest = norm(tokens, own, moe_gain[None, :], sums, span)
    wide = residual.astype(jnp.float32)

    same = [chip_exchange(first, s) for s in range(chips)]
    blocks = same + [exchange(jnp.concatenate(same, axis=0), "ctx", 1)]
    rest = lax.all_gather(rest, "ctx", axis=0, tiled=True)
    rows = pick_rows(order, pick, blocks, peers)
    parts = []
    for c in range(CHUNKS):
        if c:
            rows = pick_rows(order, pick, [rest], peers, c - 1, CHUNKS - 1)
        sent = {k: exchange(rows[k], "grp", k) for k in turn}
        parts.append([sent[k] for k in range(peers)])
    carry, deps = None, [rows[0]]
    for c in range(CHUNKS):
        last = c == CHUNKS - 1
        carry = expert_hidden(
            parts[c], c * span, w_gate_experts, w_up_experts, carry, last, [] if last else deps
        )
    hidden = carry

    ready = [expert_down(hidden, w_down_experts, c, CHUNKS, peers) for c in range(CHUNKS)]
    early = CHUNKS // 2
    outs, totals = [], []
    for c in range(CHUNKS):
        sent = {k: exchange(ready[c][k], "grp", k) for k in turn}
        back = [sent[k] for k in range(peers)]
        if c < early:
            deps = [r[0] for r in ready[c + 1 :]]
            totals.append(mix_rows(order, mix, back, jnp.bfloat16, deps=deps))
            if c < early - 1:
                continue
            total = jnp.concatenate(totals, axis=1)
            total = lax.psum_scatter(total, "ctx", scatter_dimension=0, tiled=True)
            total = wide[:, : early * span] + total.astype(jnp.float32)
        else:
            other = mix_rows(order, mix, back, jnp.bfloat16, chips, chips, outs[1:])
            other = exchange(other, "ctx", 1)
            both = mix_rows(order, mix, back, jnp.float32, 0, chips) + other.astype(jnp.float32)
            total = wide[:, c * span : (c + 1) * span] + both[:tok_count]
            for s in range(1, chips):
                piece = both[s * tok_count : (s + 1) * tok_count].astype(jnp.bfloat16)
                total = total + chip_exchange(piece, s).astype(jnp.float32)
        outs.append(total.astype(jnp.bfloat16))
    return jnp.concatenate(outs, axis=1)


def solution(mesh):
    return jax.shard_map(
        per_device,
        mesh=mesh,
        in_specs=(
            P(("grp", "ctx"), None),
            P(("grp", "ctx"), None),
            P("grp", "ctx", None),
            P("grp", None),
            P(),
            P(("grp", "ctx"), None),
            P(("grp", "ctx"), None),
            P(("grp", "ctx"), None, None),
            P(("grp", "ctx"), None, None),
            P(("grp", "ctx"), None, None),
        ),
        out_specs=P(("grp", "ctx"), None),
        check_vma=False,
    )
```

```python
import functools
import math

import jax
import jax.numpy as jnp
from jax import lax
from jax.experimental import pallas as pl
from jax.experimental.pallas import tpu as pltpu
from jax.sharding import PartitionSpec as P

H = 32
KV_HEADS = 4
HEAD_DIM = 128
EXPERTS = 128
TOPK = 8
CAP = 12

CHUNKS = 4
VMEM_LIMIT = 24 * 1024 * 1024
VMEM_MOST = 60 * 1024 * 1024


def call(kernel, deps, operands, in_specs, vmem=VMEM_LIMIT, **kwargs):
    count = len(operands)

    def run(*refs):
        kernel(*refs[:count], *refs[count + len(deps) :])

    in_specs = in_specs + [pl.BlockSpec(memory_space=pl.ANY)] * len(deps)
    params = pltpu.CompilerParams(vmem_limit_bytes=vmem)
    if "grid_spec" in kwargs:
        kwargs["grid_spec"] = kwargs["grid_spec"](in_specs)
        in_specs = None
    else:
        kwargs["in_specs"] = in_specs
    return pl.pallas_call(run, compiler_params=params, **kwargs)(*operands, *deps)


def attention_kernel(where_ref, q_ref, *refs, blocks, stack, old):
    k_refs, v_refs = refs[: blocks + 1], refs[blocks + 1 : 2 * blocks + 2]
    o_ref, key_ref, value_ref = refs[2 * blocks + 2 :]
    rows, wide = q_ref.shape
    keys = key_ref.shape[0]
    span, lead = keys // blocks, k_refs[0].shape[0] // blocks
    factor = math.log2(math.e) / math.sqrt(HEAD_DIM)
    for b in range(blocks):
        at = slice(b * span, b * span + lead)
        part = slice(b * lead, (b + 1) * lead)
        key_ref[at, :] = k_refs[0][part, :]
        value_ref[at, :HEAD_DIM] = v_refs[0][part, :]
        at = pl.ds(pl.multiple_of(where_ref[3 + b] * span + lead, lead), span - lead)
        key_ref[at, :] = k_refs[1 + b][...]
        value_ref[at, :HEAD_DIM] = v_refs[1 + b][...]
    value_ref[:, HEAD_DIM:] = jnp.ones((keys, HEAD_DIM), value_ref.dtype)
    late = (stack * rows, keys - old)
    row = lax.broadcasted_iota(jnp.int32, late, 0) % rows
    allowed = lax.broadcasted_iota(jnp.int32, late, 1) + old <= row + where_ref[2]
    for first in range(0, wide // HEAD_DIM, stack):
        query = jnp.concatenate(
            [q_ref[:, h * HEAD_DIM : (h + 1) * HEAD_DIM] for h in range(first, first + stack)],
            axis=0,
        )
        scores = lax.dot_general(
            query, key_ref[...], (((1,), (1,)), ((), ())), preferred_element_type=jnp.float32
        )
        scores = jnp.concatenate(
            [scores[:, :old], jnp.where(allowed, scores[:, old:], -1e30)], axis=1
        )
        top = jnp.max(scores, axis=1, keepdims=True)
        weights = jnp.exp2((scores - top) * factor).astype(jnp.bfloat16)
        summed = jnp.dot(weights, value_ref[...], preferred_element_type=jnp.float32)
        out = (summed[:, :HEAD_DIM] / summed[:, HEAD_DIM:]).astype(o_ref.dtype)
        for i in range(stack):
            h = first + i
            o_ref[:, h * HEAD_DIM : (h + 1) * HEAD_DIM] = out[i * rows : (i + 1) * rows]


def attention(queries, kv_lead, kv_blocks, span, where, old, peers, deps):
    rows = queries.shape[0]
    wide = queries.shape[1] // peers
    blocks = len(kv_blocks)
    keys = blocks * span
    lead = kv_lead.shape[0] // blocks

    def column(size, first):
        return pl.BlockSpec((size, HEAD_DIM), lambda i, where: (0, first + where[1]))

    sizes = [lead * blocks] + [span - lead] * blocks
    return call(
        functools.partial(attention_kernel, blocks=blocks, stack=2, old=old),
        deps,
        [where, queries] + [kv_lead, *kv_blocks] * 2,
        [pl.BlockSpec((rows, wide), lambda i, where: (0, where[0]))]
        + [column(size, 0) for size in sizes]
        + [column(size, KV_HEADS) for size in sizes],
        grid_spec=lambda in_specs: pltpu.PrefetchScalarGridSpec(
            num_scalar_prefetch=1,
            grid=(1,),
            in_specs=in_specs,
            out_specs=pl.BlockSpec((rows, wide), lambda i, where: (0, 0)),
            scratch_shapes=[
                pltpu.VMEM((keys, HEAD_DIM), jnp.bfloat16),
                pltpu.VMEM((keys, 2 * HEAD_DIM), jnp.bfloat16),
            ],
        ),
        out_shape=jax.ShapeDtypeStruct((rows, wide), jnp.bfloat16),
        cost_estimate=pl.CostEstimate(
            flops=4 * rows * wide * keys,
            bytes_accessed=4 * (keys * HEAD_DIM + rows * wide),
            transcendentals=rows * wide // HEAD_DIM * keys,
        ),
        name="attention",
        vmem=51 * 1024 * 1024,
    )


def pick_kernel(order_ref, pick_ref, *refs, blocks):
    if blocks > 1:
        block_refs, outs, scratch = refs[:blocks], refs[blocks:-1], refs[-1]
        span = block_refs[0].shape[0]
        number = 0
        for ref in block_refs:
            for part in range(ref.shape[0] // span):
                at = pl.ds(pl.multiple_of(order_ref[number] * span, span), span)
                scratch[at, :] = ref[part * span : (part + 1) * span, :]
                number += 1
        block = scratch[...]
    else:
        block, outs = refs[0][...], refs[1:]
    count = outs[0].shape[0]
    for k, out in enumerate(outs):
        out[...] = jnp.dot(
            pick_ref[k * count : (k + 1) * count, :], block, preferred_element_type=jnp.float32
        ).astype(out.dtype)


def pick_rows(order, pick, blocks, peers, chunk=0, chunks=1):
    count, width = pick.shape[0] // peers, blocks[0].shape[1] // chunks

    def whole(shape):
        return pl.BlockSpec(shape, lambda i: (0, 0))

    return call(
        functools.partial(pick_kernel, blocks=len(blocks)),
        [],
        [order, pick, *blocks],
        [pl.BlockSpec(memory_space=pltpu.SMEM), whole(pick.shape)]
        + [pl.BlockSpec((b.shape[0], width), lambda i: (0, chunk)) for b in blocks],
        grid=(1,),
        out_specs=[whole((count, width))] * peers,
        out_shape=[jax.ShapeDtypeStruct((count, width), jnp.bfloat16)] * peers,
        scratch_shapes=[pltpu.VMEM((pick.shape[1], width), jnp.bfloat16)] * (len(blocks) > 1),
        cost_estimate=pl.CostEstimate(
            flops=2 * pick.size * width,
            bytes_accessed=2 * (pick.size + (pick.shape[0] + pick.shape[1]) * width),
            transcendentals=0,
        ),
        name="pick_rows",
        vmem=48 * 1024 * 1024,
    )


def hidden_kernel(*refs, peers, carried, last):
    x_refs, refs = refs[:peers], refs[peers:]
    gate_ref, up_ref, *refs = refs
    part = jnp.concatenate([x[...] for x in x_refs], axis=0)
    gate = jnp.dot(part, gate_ref[0], preferred_element_type=jnp.float32)
    up = jnp.dot(part, up_ref[0], preferred_element_type=jnp.float32)
    if carried:
        gate = gate + refs[0][0]
        up = up + refs[1][0]
        refs = refs[2:]
    if last:
        refs[0][0] = (gate / (1.0 + jnp.exp(-gate)) * up).astype(refs[0].dtype)
    else:
        refs[0][0] = gate
        refs[1][0] = up


def expert_hidden(part, first, w_gate, w_up, carry, last, deps=()):
    peers = len(part)
    width = part[0].shape[1]
    local, _, inner = w_gate.shape
    slots = part[0].shape[0] // local
    rows = peers * slots
    assert first % width == 0
    weight_spec = pl.BlockSpec((1, width, inner), lambda j: (j, first // width, 0))
    sum_spec = pl.BlockSpec((1, rows, inner), lambda j: (j, 0, 0))
    total = jax.ShapeDtypeStruct((local, rows, inner), jnp.float32)
    return call(
        functools.partial(hidden_kernel, peers=peers, carried=carry is not None, last=last),
        deps,
        [*part, w_gate, w_up, *(carry or ())],
        [pl.BlockSpec((slots, width), lambda j: (j, 0))] * peers
        + [weight_spec] * 2
        + ([] if carry is None else [sum_spec] * 2),
        grid=(local,),
        out_specs=sum_spec if last else [sum_spec] * 2,
        out_shape=jax.ShapeDtypeStruct(total.shape, jnp.bfloat16) if last else [total] * 2,
        cost_estimate=pl.CostEstimate(
            flops=4 * local * rows * width * inner,
            bytes_accessed=4 * local * width * inner + 10 * local * rows * inner,
            transcendentals=local * rows * inner,
        ),
        name="expert_hidden",
        vmem=24 * 1024 * 1024,
    )


def down_kernel(h_ref, w_ref, *y_refs):
    slots = y_refs[0].shape[0]
    out = jnp.dot(h_ref[0], w_ref[0], preferred_element_type=jnp.float32).astype(jnp.bfloat16)
    for k, y_ref in enumerate(y_refs):
        y_ref[...] = out[k * slots : (k + 1) * slots]


def expert_down(hidden, w_down, chunk, chunks, peers):
    local, rows, inner = hidden.shape
    width = w_down.shape[2] // chunks
    slots = rows // peers
    return pl.pallas_call(
        down_kernel,
        grid=(local,),
        in_specs=[
            pl.BlockSpec((1, rows, inner), lambda j: (j, 0, 0)),
            pl.BlockSpec((1, inner, width), lambda j: (j, 0, chunk)),
        ],
        out_specs=[pl.BlockSpec((slots, width), lambda j: (j, 0))] * peers,
        out_shape=[jax.ShapeDtypeStruct((local * slots, width), jnp.bfloat16)] * peers,
        compiler_params=pltpu.CompilerParams(vmem_limit_bytes=48 * 1024 * 1024),
        cost_estimate=pl.CostEstimate(
            flops=2 * local * rows * width * inner,
            bytes_accessed=2 * local * (inner * width + rows * (inner + width)),
            transcendentals=0,
        ),
        name="expert_down",
    )(hidden, w_down)


def mix_kernel(order_ref, mix_ref, *refs, first, count):
    rows = jnp.concatenate([r[...] for r in refs[:-1]], axis=0)
    if count:
        span = refs[-1].shape[0] // count
        mix = jnp.concatenate(
            [
                mix_ref[pl.ds(pl.multiple_of(order_ref[first + i] * span, span), span), :]
                for i in range(count)
            ],
            axis=0,
        )
    else:
        mix = mix_ref[...]
    out = jnp.dot(mix, rows, preferred_element_type=jnp.float32)
    refs[-1][...] = out.astype(refs[-1].dtype)


def mix_rows(order, mix, parts, dtype, first=0, count=0, deps=()):
    rows = mix.shape[0] * (count or len(order)) // len(order)
    width = parts[0].shape[1]
    vmem = pl.BlockSpec(memory_space=pltpu.VMEM)
    return call(
        functools.partial(mix_kernel, first=first, count=count),
        deps,
        [order, mix, *parts],
        [pl.BlockSpec(memory_space=pltpu.SMEM)] + [vmem] * (1 + len(parts)),
        out_specs=vmem,
        out_shape=jax.ShapeDtypeStruct((rows, width), dtype),
        cost_estimate=pl.CostEstimate(
            flops=2 * rows * mix.shape[1] * width,
            bytes_accessed=2 * (mix.size + (mix.shape[0] + mix.shape[1]) * width),
            transcendentals=0,
        ),
        name="mix_rows",
        vmem=24 * 1024 * 1024,
    )


def table_kernel(order_ref, place_ref, gate_ref, pick_ref, mix_ref, *, slots):
    group, local, column = place_ref.shape
    blocks = order_ref.shape[0]
    span = column // blocks
    slot = lax.broadcasted_iota(jnp.int32, (slots, span), 0)
    for b in range(blocks):
        here = slice(b * span, (b + 1) * span)
        hits, gates = [], []
        for g in range(group):
            for j in range(local):
                hit = place_ref[g, j : j + 1, here] == slot
                hits.append(jnp.where(hit, 1.0, 0.0))
                gates.append(jnp.where(hit, gate_ref[g, j : j + 1, here], 0.0))
        at = pl.ds(pl.multiple_of(order_ref[b] * span, span), span)
        pick_ref[:, at] = jnp.concatenate(hits, axis=0).astype(pick_ref.dtype)
        mix_ref[at, :] = jnp.concatenate(gates, axis=0).T.astype(mix_ref.dtype)


def tables(order, place, gate, slots):
    peers, local, column = place.shape
    rows = local * slots
    group = next(g for g in range(1, peers + 1) if g == peers or not (peers % g or g * rows % 128))
    return pl.pallas_call(
        functools.partial(table_kernel, slots=slots),
        grid=(peers // group,),
        in_specs=[pl.BlockSpec(memory_space=pltpu.SMEM)]
        + [pl.BlockSpec((group, local, column), lambda k: (k, 0, 0))] * 2,
        out_specs=[
            pl.BlockSpec((group * rows, column), lambda k: (k, 0)),
            pl.BlockSpec((column, group * rows), lambda k: (0, k)),
        ],
        out_shape=[
            jax.ShapeDtypeStruct((peers * rows, column), jnp.bfloat16),
            jax.ShapeDtypeStruct((column, peers * rows), jnp.bfloat16),
        ],
        compiler_params=pltpu.CompilerParams(vmem_limit_bytes=48 * 1024 * 1024),
        cost_estimate=pl.CostEstimate(
            flops=4 * peers * rows * column,
            bytes_accessed=4 * peers * rows * column,
            transcendentals=0,
        ),
        name="tables",
    )(order, place, gate)


def norm_kernel(tokens_ref, own_ref, gain_ref, *refs):
    *part_refs, res_ref, first_ref, rest_ref = refs
    width, span = tokens_ref.shape[1], first_ref.shape[1]
    total = own_ref[...]
    for ref in part_refs:
        total = total + ref[...].astype(jnp.float32)
    res = (tokens_ref[...].astype(jnp.float32) + total).astype(res_ref.dtype)
    res_ref[...] = res
    res = res.astype(jnp.float32)
    mean = jnp.sum(res * res, axis=1, keepdims=True) * (1.0 / width)
    normed = (res * lax.rsqrt(mean + 1e-06) * gain_ref[...]).astype(first_ref.dtype)
    first_ref[...] = normed[:, :span]
    rest_ref[...] = normed[:, span:]


def norm(tokens, own, gain, parts, span):
    rows, width = tokens.shape
    vmem = pl.BlockSpec(memory_space=pltpu.VMEM)
    operands = [tokens, own, gain, *parts]
    return call(
        norm_kernel,
        [],
        operands,
        [vmem] * len(operands),
        out_specs=[vmem] * 3,
        out_shape=[
            jax.ShapeDtypeStruct((rows, size), jnp.bfloat16) for size in (width, span, width - span)
        ],
        name="norm",
    )


def exchange(value, axis, k):
    if k == 0:
        return value
    return lax.ppermute(value, axis, [(i, i ^ k) for i in range(lax.axis_size(axis))])


def chip_exchange(value, turn):
    if turn == 0:
        return value
    count = lax.axis_size("ctx")
    steps = (2 * turn, count - 2 * turn)
    return lax.ppermute(value, "ctx", [(i, i ^ steps[i % 2]) for i in range(count)])


def per_device(
    tokens,
    queries,
    keys_values,
    out_weight,
    moe_gain,
    expert_ids,
    gates,
    w_gate_experts,
    w_up_experts,
    w_down_experts,
):
    tok_count, width = tokens.shape
    ctx_count = lax.axis_size("ctx")
    peers = lax.axis_size("grp")
    chips = ctx_count // 2
    here, me = lax.axis_index("ctx"), lax.axis_index("grp")
    local = w_gate_experts.shape[0]
    slots = ctx_count * CAP
    column = ctx_count * tok_count
    turn = [k for k in reversed(range(peers))]

    turns = 2 * jnp.arange(chips, dtype=jnp.int32)
    back_turns = (ctx_count - turns) % ctx_count
    even = here % 2 == 0
    order = here ^ jnp.concatenate(
        [
            jnp.where(even, turns, back_turns),
            jnp.where(even, back_turns, turns) + 1,
        ]
    )

    kv_span = keys_values.shape[1]
    lead = kv_span // 2
    routes = jnp.concatenate([expert_ids.astype(jnp.bfloat16), gates.astype(jnp.bfloat16)], axis=1)
    routes = jnp.pad(routes.T, ((0, 0), (0, keys_values.shape[2] - tok_count)))
    block = jnp.concatenate([keys_values[0, lead:], routes], axis=0)
    kv_same = [chip_exchange(block, s) for s in reversed(range(chips))][::-1]
    kv_lead = lax.all_gather(keys_values[0, :lead], "ctx", axis=0, tiled=True)
    kv_blocks = kv_same + [exchange(b, "ctx", 1) for b in kv_same]

    routes = jnp.concatenate([b[kv_span - lead :, :tok_count] for b in kv_blocks], axis=1).astype(jnp.float32)
    ids, gate_rows = routes[:TOPK].astype(jnp.int32), routes[TOPK:]
    owner = me ^ jnp.arange(peers, dtype=jnp.int32)
    wanted = (
        ((owner * ctx_count + here) * local)[:, None] + jnp.arange(local, dtype=jnp.int32)[None, :]
    ).reshape(-1)
    same = ids[None, :, :] == wanted[:, None, None]
    named = jnp.any(same, axis=1)
    gate_of = jnp.sum(jnp.where(same, gate_rows[None], 0.0), axis=1)
    earlier = jnp.triu(jnp.ones((tok_count, tok_count), jnp.bfloat16), 1)
    rank = jnp.dot(
        named.reshape(-1, tok_count).astype(jnp.bfloat16),
        earlier,
        preferred_element_type=jnp.float32,
    ).astype(jnp.int32)
    place = rank.reshape(-1, column) + jnp.repeat(order * CAP, tok_count)
    place = jnp.where(named, place, -1)
    pick, mix = tables(
        order, place.reshape(peers, local, column), gate_of.reshape(peers, local, column), slots
    )

    old = keys_values.shape[1] * ctx_count - column
    heads = H // peers
    sent, deps = {}, []
    for k in turn:
        peer = me ^ k
        where = jnp.concatenate(
            [
                jnp.stack([peer, peer * heads // (H // KV_HEADS), old + here * tok_count]).astype(
                    jnp.int32
                ),
                order,
            ]
        )
        if k == 0:
            deps = [
                jnp.dot(sent[j], out_weight, preferred_element_type=jnp.float32).astype(jnp.bfloat16)
                for j in turn[:-1]
            ]
            sums = [exchange(d, "grp", j) for j, d in zip(turn[:-1], deps)]
            deps = deps + [pick, mix]
        attended = attention(queries, kv_lead, kv_blocks, kv_span, where, old, peers, deps)
        sent[k] = exchange(attended, "grp", k)
    own = jnp.dot(sent[0], out_weight, preferred_element_type=jnp.float32)
    span = width // CHUNKS
    residual, first, rest = norm(tokens, own, moe_gain[None, :], sums, span)
    wide = residual.astype(jnp.float32)

    same = [chip_exchange(first, s) for s in range(chips)]
    blocks = same + [exchange(jnp.concatenate(same, axis=0), "ctx", 1)]
    rest = lax.all_gather(rest, "ctx", axis=0, tiled=True)
    rows = pick_rows(order, pick, blocks, peers)
    parts = []
    for c in range(CHUNKS):
        if c:
            rows = pick_rows(order, pick, [rest], peers, c - 1, CHUNKS - 1)
        sent = {k: exchange(rows[k], "grp", k) for k in turn}
        parts.append([sent[k] for k in range(peers)])
    carry, deps = None, [rows[0]]
    for c in range(CHUNKS):
        last = c == CHUNKS - 1
        carry = expert_hidden(
            parts[c], c * span, w_gate_experts, w_up_experts, carry, last, [] if last else deps
        )
    hidden = carry

    ready = [expert_down(hidden, w_down_experts, c, CHUNKS, peers) for c in range(CHUNKS)]
    early = CHUNKS // 2
    outs, totals = [], []
    for c in range(CHUNKS):
        sent = {k: exchange(ready[c][k], "grp", k) for k in turn}
        back = [sent[k] for k in range(peers)]
        if c < early:
            deps = [r[0] for r in ready[c + 1 :]]
            totals.append(mix_rows(order, mix, back, jnp.bfloat16, deps=deps))
            if c < early - 1:
                continue
            total = jnp.concatenate(totals, axis=1)
            total = lax.psum_scatter(total, "ctx", scatter_dimension=0, tiled=True)
            total = wide[:, : early * span] + total.astype(jnp.float32)
        else:
            other = mix_rows(order, mix, back, jnp.bfloat16, chips, chips, outs[1:])
            other = exchange(other, "ctx", 1)
            both = mix_rows(order, mix, back, jnp.float32, 0, chips) + other.astype(jnp.float32)
            total = wide[:, c * span : (c + 1) * span] + both[:tok_count]
            for s in range(1, chips):
                piece = both[s * tok_count : (s + 1) * tok_count].astype(jnp.bfloat16)
                total = total + chip_exchange(piece, s).astype(jnp.float32)
        outs.append(total.astype(jnp.bfloat16))
    return jnp.concatenate(outs, axis=1)


def solution(mesh):
    return jax.shard_map(
        per_device,
        mesh=mesh,
        in_specs=(
            P(("grp", "ctx"), None),
            P(("grp", "ctx"), None),
            P("grp", "ctx", None),
            P("grp", None),
            P(),
            P(("grp", "ctx"), None),
            P(("grp", "ctx"), None),
            P(("grp", "ctx"), None, None),
            P(("grp", "ctx"), None, None),
            P(("grp", "ctx"), None, None),
        ),
        out_specs=P(("grp", "ctx"), None),
        check_vma=False,
    )
```
